256 devices in a mesh: ctx: 2 (over core), head: 4 (over x), sess: 32 (over z, y).
Axes of the slice: x: 4, y: 4, z: 8, core: 2. Of those that a mesh axis runs over, the one named last changes fastest.
Arguments:
- queries: bfloat16 [32, 512, 16, 128], P('sess', 'ctx', 'head'), may hold values from -6 to 6
- keys: bfloat16 [32, 512, 16, 128], P('sess', 'ctx', 'head'), may hold values from -6 to 6
- values: bfloat16 [32, 512, 32, 128], P('sess', 'ctx', 'head'), may hold values from -6 to 6
- gate_logit: float32 [32, 32, 512], P('sess', 'head', 'ctx'), may hold values from -10.1 to 0
- beta_logit: float32 [32, 32, 512], P('sess', 'head', 'ctx'), may hold values from -6 to 6
- token_blocks: int32 [32], P('sess'), may hold values from 1 to 4, as said below
- slot_map: int32 [32], replicated, may hold values from 0 to 31, as said below
Outputs:
- token_out: bfloat16 [32, 512, 32, 128], P('sess', 'ctx', 'head')
- slot_states: float32 [32, 32, 128, 128], P('sess', 'head', 'ctx')
The draws below stay inside these ranges and needn't reach their ends.
Inputs may be any that keep to these rules, and one draw needn't show every extreme that they name: `token_blocks`: one session reaches the largest length in every draw. slot_map is a permutation of the slots; slot j belongs to index j // 1 of sess.
All inputs are finite; a program needn't handle non-finite values.
Results may differ from the reference program's by a relative error of at most 0.0011.
Values sent between devices are 32-bit elements; how exact they have to be, the bound alone decides.
No kernel may reach another device: no remote copies, remote signals or barrier semaphores. Data moves between devices by JAX's collectives and lax.ppermute only.
A program may use at most 64 MiB of HBM per device.

```python
import jax
import jax.numpy as jnp
from jax import lax

DK = 128
DV = 128
QK_HEADS = 16
VALUE_HEADS = 32
TOK_DEV = 256
BLOCK = 128
SESSION_TOKENS = 512
SESSION_TOTAL = 32


def draw_gate_logit(key, part):
    key = jax.random.fold_in(key, 11)
    session_flows = jax.random.split(key, 7)
    fast_share = 0.5
    fast = jax.random.uniform(session_flows[0], (SESSION_TOTAL, VALUE_HEADS, 1)) < fast_share
    base_fast = jax.random.uniform(session_flows[1], (SESSION_TOTAL, VALUE_HEADS, 1), minval=-3.9, maxval=-3.4)
    base_slow = jax.random.uniform(session_flows[2], (SESSION_TOTAL, VALUE_HEADS, 1), minval=-9.0, maxval=-8.3)
    base_decay = jnp.where(fast, base_fast, base_slow)
    device_offset = jax.random.uniform(session_flows[3], (SESSION_TOTAL, VALUE_HEADS, SESSION_TOKENS // TOK_DEV), minval=-0.35, maxval=0.35)
    device_offset = jnp.repeat(device_offset, TOK_DEV, axis=2)
    random_noise = jax.random.uniform(session_flows[4], (SESSION_TOTAL, VALUE_HEADS, SESSION_TOKENS), minval=-0.7, maxval=0.7)
    spike_position = jax.random.randint(session_flows[5], (SESSION_TOTAL, VALUE_HEADS, 2), 0, SESSION_TOKENS)
    slot_places = jnp.arange(SESSION_TOKENS, dtype=jnp.int32)
    spiked_tokens = jnp.any(slot_places[None, None, :, None] == spike_position[:, :, None, :], axis=-1)
    spike_strength = jax.random.uniform(session_flows[6], (SESSION_TOTAL, VALUE_HEADS, SESSION_TOKENS), minval=-1.4, maxval=0.0)
    return jnp.where(spiked_tokens, spike_strength, base_decay + device_offset + random_noise).astype(jnp.float32)


def draw_token_blocks(key, part):
    key = jax.random.fold_in(key, 23)
    first, second = jax.random.split(key)
    most = SESSION_TOKENS // BLOCK
    blocks = jax.random.randint(first, (SESSION_TOTAL,), 1, most + 1)
    chosen = jax.random.randint(second, (), 0, SESSION_TOTAL)
    return jnp.where(jnp.arange(SESSION_TOTAL) == chosen, most, blocks).astype(jnp.int32)


def force_pair(order, position, target):
    places = jnp.arange(SESSION_TOTAL, dtype=jnp.int32)
    holder = jnp.argmax((order == target).astype(jnp.int32)).astype(jnp.int32)
    held = order[position]
    order = jnp.where(places == holder, held, order)
    order = jnp.where(places == position, target, order)
    return order


def draw_slot_map(key, part):
    key = jax.random.fold_in(key, 37)
    first, second = jax.random.split(key)
    total = SESSION_TOTAL
    order = jax.random.permutation(first, total).astype(jnp.int32)
    anchor = jax.random.randint(second, (), 0, total).astype(jnp.int32)
    order = force_pair(order, anchor, (anchor + 1) % total)
    order = force_pair(order, (anchor + 2) % total, (anchor + 2 + total // 2) % total)
    if total >= 8:
        order = force_pair(order, (anchor + 5) % total, (anchor + 4) % total)
    return order.astype(jnp.int32)


def levels(own_key, dims, pieces, smallest, high):
    def one(dim, parts):
        steps = jax.random.uniform(jax.random.fold_in(jax.random.fold_in(own_key, 6), dim), (parts,), jnp.float32, smallest / len(pieces), high / len(pieces))
        return jnp.repeat(jnp.exp(steps), dims[dim] // parts).reshape((-1,) + (1,) * (len(dims) - dim - 1))

    level = one(*pieces[0])
    for cut in pieces[1:]:
        level = level * one(*cut)
    return level


def normal_values(own_key, extent, deviation, reach, cuts=(), kind=jnp.bfloat16):
    array = deviation * jax.random.normal(own_key, extent, jnp.float32)
    if cuts:
        array = array * levels(own_key, extent, cuts, -0.22, 0.18)
    return jnp.clip(array, -reach, reach).astype(kind)


def setup_inputs(seed: int = 0) -> dict:
    seeds = jax.random.split(jax.random.key(seed), 8)
    queries = normal_values(seeds[0], (SESSION_TOTAL, SESSION_TOKENS, QK_HEADS, DK), 1.0, 6.0, ((0, 32), (1, 2), (2, 4)))
    keys = normal_values(seeds[1], (SESSION_TOTAL, SESSION_TOKENS, QK_HEADS, DK), 1.0, 6.0, ((0, 32), (1, 2), (2, 4)))
    values = normal_values(seeds[2], (SESSION_TOTAL, SESSION_TOKENS, VALUE_HEADS, DV), 1.0, 6.0, ((0, 32), (1, 2), (2, 4)))
    gate_logit = draw_gate_logit(jax.random.fold_in(seeds[7], 71), 0)
    beta_logit = normal_values(seeds[4], (SESSION_TOTAL, VALUE_HEADS, SESSION_TOKENS), 1.5, 6.0, ((0, 32), (1, 4), (2, 2)), jnp.float32)
    token_blocks = draw_token_blocks(jax.random.fold_in(seeds[7], 71), 0)
    slot_map = draw_slot_map(jax.random.fold_in(seeds[7], 71), 0)
    return dict(queries=queries, keys=keys, values=values, gate_logit=gate_logit, beta_logit=beta_logit, token_blocks=token_blocks, slot_map=slot_map)


HIGH_PRECISION = lax.Precision.HIGHEST

def unit_rows(x):
    x = x.astype(jnp.float32)
    return x * lax.rsqrt(lax.optimization_barrier(jnp.sum(x * x, axis=-1, keepdims=True)) + 1e-06)

def one_session(packed):
    qn, kn, vf, alpha, beta = packed

    def advance(recurrent_state, items):
        query_vector, key_vector, value, decay, write = items
        state_readout = jnp.einsum('nm,nmj->nj', key_vector, recurrent_state, precision=HIGH_PRECISION)
        delta = write[:, None] * (value - decay[:, None] * state_readout)
        recurrent_state = decay[:, None, None] * recurrent_state + key_vector[:, :, None] * delta[:, None, :]
        final_result = jnp.einsum('nm,nmj->nj', query_vector, recurrent_state, precision=HIGH_PRECISION)
        return (recurrent_state, final_result)
    start = jnp.zeros((VALUE_HEADS, DK, DV), jnp.float32)
    final, outputs = lax.scan(advance, start, (qn, kn, vf, alpha.T, beta.T))
    return (final, outputs)

def reference(queries, keys, values, gate_logit, beta_logit, token_blocks, slot_map):
    group = VALUE_HEADS // QK_HEADS
    qn = jnp.repeat(unit_rows(queries), group, axis=2)
    kn = jnp.repeat(unit_rows(keys), group, axis=2)
    vf = values.astype(jnp.float32)
    slot_places = jnp.arange(SESSION_TOKENS, dtype=jnp.int32)
    live = slot_places[None, :] < (token_blocks * BLOCK)[:, None]
    alpha = jnp.where(live[:, None, :], jnp.exp(-jax.nn.softplus(gate_logit)), 1.0)
    beta = jnp.where(live[:, None, :], jax.nn.sigmoid(beta_logit), 0.0)
    finals, outputs = lax.map(one_session, (qn, kn, vf, alpha, beta))
    token_out = jnp.where(live[:, :, None, None], outputs, 0.0).astype(jnp.bfloat16)
    owners = jnp.argsort(slot_map).astype(jnp.int32)
    slot_states = finals[owners]
    return (token_out, slot_states)
```

```python
import functools
import jax
import jax.numpy as jnp
from jax import lax
from jax.experimental import pallas as pl
from jax.experimental.pallas import tpu as pltpu

F32 = jnp.float32
BF16 = jnp.bfloat16


def split(x):
    hi = x.astype(BF16)
    return hi, (x - hi.astype(F32)).astype(BF16)


def mm(a, b):
    return jnp.dot(a, b, preferred_element_type=F32)


def mm_nt(a, b):
    return lax.dot_general(a, b, (((1,), (1,)), ((), ())), preferred_element_type=F32)


def pack_left(a):
    hi, lo = split(a)
    return jnp.concatenate([hi, lo], axis=1)


def pack_right(b):
    hi, lo = split(b)
    row = jnp.concatenate([hi, lo], axis=1)
    return jnp.concatenate([row, row], axis=0)


def fold(r):
    return r[:, :128] + r[:, 128:]


def mm_small(a, b):
    return fold(mm(pack_left(a), pack_right(b)))


def mm_wide(a, b):
    ah, al = split(a)
    bh, bl = split(b)
    return mm(jnp.concatenate([ah, al], axis=1), jnp.concatenate([bh, bh], axis=0)) + mm(ah, bl)


def decay_rows(gate, live):
    x = jnp.where(live, -(jnp.maximum(gate, 0.0) + jnp.log1p(jnp.exp(-jnp.abs(gate)))), 0.0)
    lane = lax.broadcasted_iota(jnp.int32, x.shape, 1)
    step = 1
    while step < 256:
        x = x + jnp.where(lane >= step, pltpu.roll(x, step, 1), 0.0)
        step *= 2
    return x


def to_columns(rows):
    pad = jnp.zeros((128 - rows.shape[0], 256), F32)
    return jnp.concatenate([rows, pad], axis=0).T


def live_lanes(info_ref):
    edge = info_ref[1] * 128 - info_ref[0] * 256
    return lax.broadcasted_iota(jnp.int32, (8, 256), 1) < edge


def log_norm(x):
    return -0.5 * jnp.log(jnp.sum(x * x, axis=1, keepdims=True) + 1e-06)


def maps_kernel(
    info_ref, k_ref, v_ref, g_ref, b_ref, pay_ref, keep_ref, y_ref,
    kf, vf, acol, rcol, bcol, zcol, brow, gend, l11, l21, l22, cmp_ref, xc,
):
    kf[...] = k_ref[...].astype(F32)
    vf[...] = v_ref[...].astype(F32)
    live = live_lanes(info_ref)
    G = decay_rows(g_ref[...], live)
    logit = b_ref[...]
    beta = jnp.where(live, 1.0 / (1.0 + jnp.exp(-logit)), 0.0)
    cols = to_columns(jnp.concatenate([G, beta], axis=0))
    lane = lax.broadcasted_iota(jnp.int32, (256, 128), 1)
    norms = jnp.zeros((256, 128), F32)
    for kh in range(4):
        x = kf[pl.ds(kh, 256, stride=4), :]
        norms = jnp.where(lane == kh, log_norm(x), norms)
    norm_rows = norms.T
    for h in range(8):
        kh = h // 2
        g_c = cols[:, h : h + 1]
        be_c = cols[:, 8 + h : 9 + h]
        n_c = norms[:, kh : kh + 1]
        a = g_c + jnp.log(be_c) + n_c
        acol[h] = jnp.broadcast_to(a, (256, 128))
        rcol[h] = jnp.broadcast_to(jnp.exp(a), (256, 128))
        bcol[h] = jnp.broadcast_to(be_c, (256, 128))
        last = G[h : h + 1, 255:256]
        zcol[h] = jnp.broadcast_to(jnp.exp(last - g_c + n_c), (256, 128))
        brow[h] = jnp.broadcast_to(G[h : h + 1, :] - norm_rows[kh : kh + 1, :], (8, 256))
        gend[h] = jnp.broadcast_to(jnp.exp(last), (8, 128))

    row = lax.broadcasted_iota(jnp.int32, (128, 128), 0)
    col = lax.broadcasted_iota(jnp.int32, (128, 128), 1)
    lower = row > col

    def build(kh, c):
        k = kf[pl.ds(kh, 256, stride=4), :].astype(BF16)
        k1, k2 = k[:128], k[128:]
        kk1 = mm_nt(k1, k1)
        kk2 = mm_nt(k2, k)
        for s in range(2):
            h = 2 * kh + s
            a1, a2 = acol[h, :128], acol[h, 128:]
            b1, b2 = brow[h, 0:1, :128], brow[h, 0:1, 128:]
            l11[h] = jnp.where(lower, jnp.exp(a1 - b1) * kk1, 0.0)
            l21[h] = jnp.exp(a2 - b1) * kk2[:, :128]
            l22[h] = jnp.where(lower, jnp.exp(a2 - b2) * kk2[:, 128:], 0.0)
        return c

    lax.fori_loop(0, 4, build, 0)

    group = lax.broadcasted_iota(jnp.int32, (32, 128), 1) // 32
    for half in range(2):
        for kb in range(8):
            src = l11 if kb < 4 else l22
            r0 = (kb % 4) * 32
            acc = jnp.zeros((32, 128), F32)
            for q in range(4):
                t = src[half * 4 + q, r0 : r0 + 32, :]
                shift = (q * 32 - r0) % 128
                if shift:
                    t = pltpu.roll(t, shift, 1)
                acc = jnp.where(group == q, t, acc)
            cmp_ref[half, kb * 32 : kb * 32 + 32, :] = acc

    lane8 = lax.broadcasted_iota(jnp.int32, (8, 128), 1)
    base = (lane8 // 32) * 32
    inner = lane8 % 32
    for half in range(2):
        xs = []
        for i in range(32):
            acc = jnp.where(inner == i, 1.0, 0.0).astype(F32)
            if i:
                r = cmp_ref[half, pl.ds(i, 8, stride=32), :]
                for j in range(i):
                    coef = jnp.take_along_axis(r, base + j, axis=1, mode="promise_in_bounds")
                    acc = acc - coef * xs[j]
            xs.append(acc)
            xc[half, pl.ds(i, 8, stride=32), :] = acc

    block = row // 32 == col // 32
    odd64 = (row // 64 == col // 64) & (row // 32 != col // 32) & lower
    odd128 = (row // 64 != col // 64) & lower
    eye = row == col

    def solve(it, c):
        for s in range(HEADS_PER_STEP):
            h = it * HEADS_PER_STEP + s
            kh = h // 2
            idx = (h % 4) * 32 + col % 32
            inv = []
            for part, src in ((0, l11), (1, l22)):
                x = xc[h // 4, part * 128 : part * 128 + 128, :]
                x = jnp.take_along_axis(x, idx, axis=1, mode="promise_in_bounds")
                x = jnp.where(block, x, 0.0)
                l = src[h]
                for mask in (odd64, odd128):
                    m = mm_small(jnp.where(mask, l, 0.0), x)
                    x = x - mm_small(x, m)
                inv.append(x)
            k = kf[pl.ds(kh, 256, stride=4), :]
            v = vf[pl.ds(h, 256, stride=8), :]
            r = jnp.concatenate([rcol[h] * k, bcol[h] * v], axis=1)
            y1 = mm_wide(inv[0], r[:128])
            y2 = mm_wide(inv[1], r[128:] - mm_wide(l21[h], y1))
            y_ref[h, :128] = y1
            y_ref[h, 128:] = y2
            z = zcol[h]
            zz = jnp.concatenate([z, z], axis=1)
            zh, zl = split(zz * jnp.concatenate([y1, y2], axis=0))
            kt = k.astype(BF16).T
            st = mm(kt, zh) + mm(kt, zl)
            t = jnp.where(eye, gend[h, 0:1, :], 0.0) - st[:, :128]
            u = st[:, 128:]
            first = info_ref[0] == 0
            pay_ref[h] = jnp.where(first, u, jnp.concatenate([t[:64], u[:64]], axis=0))
            keep_ref[h] = jnp.concatenate([t[64:], u[64:]], axis=0)
        return c

    lax.fori_loop(0, 8 // HEADS_PER_STEP, solve, 0)


HEADS_PER_STEP = 4


def vm():
    return pl.BlockSpec(memory_space=pltpu.VMEM)


def sm():
    return pl.BlockSpec(memory_space=pltpu.SMEM)


def maps(info, k, v, g, b):
    big = lambda *s: pltpu.VMEM(s, F32)
    return pl.pallas_call(
        maps_kernel,
        out_shape=[
            jax.ShapeDtypeStruct((8, 128, 128), F32),
            jax.ShapeDtypeStruct((8, 128, 128), F32),
            jax.ShapeDtypeStruct((8, 256, 256), F32),
        ],
        in_specs=[sm(), vm(), vm(), vm(), vm()],
        out_specs=[vm(), vm(), vm()],
        scratch_shapes=[
            big(1024, 128), big(2048, 128),
            big(8, 256, 128), big(8, 256, 128), big(8, 256, 128), big(8, 256, 128),
            big(8, 8, 256), big(8, 8, 128),
            big(8, 128, 128), big(8, 128, 128), big(8, 128, 128),
            big(2, 256, 128), big(2, 256, 128),
        ],
        compiler_params=pltpu.CompilerParams(vmem_limit_bytes=48 * 2**20),
        name="maps",
    )(info, k, v, g, b)


def final_kernel(info_ref, pay_ref, keep_ref, got_ref, out_ref):
    def work(a_ref, m_ref):
        for h in range(8):
            out_ref[pl.ds(h * 64, 64), :] = mm_small(a_ref[h, :64], m_ref[h]) + a_ref[h, 64:]

    @pl.when(info_ref[0] == 0)
    def _():
        work(got_ref, pay_ref)

    @pl.when(info_ref[0] != 0)
    def _():
        work(keep_ref, got_ref)


def final(info, pay, keep, got):
    return pl.pallas_call(
        final_kernel,
        out_shape=jax.ShapeDtypeStruct((512, 128), F32),
        in_specs=[sm(), vm(), vm(), vm()],
        out_specs=vm(),
        compiler_params=pltpu.CompilerParams(vmem_limit_bytes=32 * 2**20),
        name="final",
    )(info, pay, keep, got)


def reads_kernel(info_ref, q_ref, k_ref, g_ref, y_ref, m_ref, o_ref, qf, kf, pcol, ecol, brow, of):
    qf[...] = q_ref[...].astype(F32)
    kf[...] = k_ref[...].astype(F32)
    G = decay_rows(g_ref[...], live_lanes(info_ref))
    cols = to_columns(G)
    lane = lax.broadcasted_iota(jnp.int32, (256, 128), 1)
    norms = jnp.zeros((256, 128), F32)
    for kh in range(4):
        norms = jnp.where(lane == kh, log_norm(kf[pl.ds(kh, 256, stride=4), :]), norms)
        norms = jnp.where(lane == 4 + kh, log_norm(qf[pl.ds(kh, 256, stride=4), :]), norms)
    norm_rows = norms.T
    for h in range(8):
        kh = h // 2
        p = cols[:, h : h + 1] + norms[:, 4 + kh : 5 + kh]
        pcol[h] = jnp.broadcast_to(p, (256, 128))
        ecol[h] = jnp.broadcast_to(jnp.exp(p), (256, 128))
        brow[h] = jnp.broadcast_to(G[h : h + 1, :] - norm_rows[kh : kh + 1, :], (8, 256))

    row = lax.broadcasted_iota(jnp.int32, (128, 128), 0)
    col = lax.broadcasted_iota(jnp.int32, (128, 128), 1)
    lower = row >= col
    has = (info_ref[0] != 0).astype(F32)
    live1 = info_ref[1] * 128 > info_ref[0] * 256
    live2 = info_ref[1] * 128 > info_ref[0] * 256 + 128

    def one(kh, c):
        k = kf[pl.ds(kh, 256, stride=4), :].astype(BF16)
        q = qf[pl.ds(kh, 256, stride=4), :].astype(BF16)
        qk1 = mm_nt(q[:128], k[:128])
        qk2 = mm_nt(q[128:], k)
        for s in range(2):
            h = 2 * kh + s
            m = m_ref[h] * has
            mh, ml = split(m)
            mrow = jnp.concatenate([mh, ml], axis=1)
            mpack = jnp.concatenate([mrow, mrow], axis=0)
            w = y_ref[h, :, :128]
            u = y_ref[h, :, 128:]
            d = u - fold(mm(pack_left(w), mpack))
            qm = fold(mm(q, mrow)) * ecol[h]
            p1, p2 = pcol[h, :128], pcol[h, 128:]
            b1, b2 = brow[h, 0:1, :128], brow[h, 0:1, 128:]
            p11 = jnp.where(lower, jnp.exp(p1 - b1) * qk1, 0.0)
            p21 = jnp.exp(p2 - b1) * qk2[:, :128]
            p22 = jnp.where(lower, jnp.exp(p2 - b2) * qk2[:, 128:], 0.0)
            o1 = qm[:128] + mm_small(p11, d[:128])
            ph, pl_ = split(jnp.concatenate([p21, p22], axis=1))
            dh, dl = split(d)
            o2 = qm[128:] + fold(mm(ph, jnp.concatenate([dh, dl], axis=1))) + mm(pl_, dh)
            o1 = jnp.where(live1, o1, 0.0)
            o2 = jnp.where(live2, o2, 0.0)
            of[pl.ds(h, 256, stride=8), :] = jnp.concatenate([o1, o2], axis=0)
        return c

    lax.fori_loop(0, 4, one, 0)
    o_ref[...] = of[...].astype(BF16)


def reads(info, q, k, g, y, m):
    big = lambda *s: pltpu.VMEM(s, F32)
    return pl.pallas_call(
        reads_kernel,
        out_shape=jax.ShapeDtypeStruct((2048, 128), BF16),
        in_specs=[sm(), vm(), vm(), vm(), vm(), vm()],
        out_specs=vm(),
        scratch_shapes=[
            big(1024, 128), big(1024, 128), big(8, 256, 128), big(8, 256, 128),
            big(8, 8, 256), big(2048, 128),
        ],
        compiler_params=pltpu.CompilerParams(vmem_limit_bytes=48 * 2**20),
        cost_estimate=pl.CostEstimate(flops=8 * 4 * 2 * 256**3, bytes_accessed=4 * 2**20, transcendentals=0),
        name="reads",
    )(info, q, k, g, y, m)


def reorder_kernel(slot_ref, in_ref, out_ref):
    for s in range(32):
        out_ref[slot_ref[s]] = in_ref[s]


def reorder(slot_map, x):
    return pl.pallas_call(
        reorder_kernel,
        out_shape=jax.ShapeDtypeStruct(x.shape, x.dtype),
        in_specs=[sm(), vm()],
        out_specs=vm(),
        name="reorder",
    )(slot_map, x)


def local(queries, keys, values, gate_logit, beta_logit, token_blocks, slot_map):
    q = queries.reshape(1024, 128)
    k = keys.reshape(1024, 128)
    v = values.reshape(2048, 128)
    g = gate_logit.reshape(8, 256)
    b = beta_logit.reshape(8, 256)
    ctx = lax.axis_index("ctx").astype(jnp.int32)
    info = jnp.stack([ctx, token_blocks[0]])
    pay, keep, y = maps(info, k, v, g, b)
    got = lax.ppermute(pay, "ctx", [(0, 1), (1, 0)])
    rows = final(info, pay, keep, got)
    spread = lax.all_to_all(rows.reshape(32, 16, 128), "sess", 0, 0, tiled=True)
    out = reads(info, q, k, g, y, got)
    back = lax.all_to_all(reorder(slot_map, spread), "sess", 0, 0, tiled=True)
    return out.reshape(1, 256, 8, 128), back.reshape(1, 8, 64, 128)


def solution(mesh):
    from jax.sharding import PartitionSpec as P
    placed = (
        P("sess", "ctx", "head", None), P("sess", "ctx", "head", None), P("sess", "ctx", "head", None),
        P("sess", "head", "ctx"), P("sess", "head", "ctx"), P("sess"), P(),
    )
    return jax.shard_map(
        local, mesh=mesh, in_specs=placed,
        out_specs=(P("sess", "ctx", "head", None), P("sess", "head", "ctx", None)),
        check_vma=False,
    )
```

```python
import functools
import jax
import jax.numpy as jnp
from jax import lax
from jax.experimental import pallas as pl
from jax.experimental.pallas import tpu as pltpu

F32 = jnp.float32
BF16 = jnp.bfloat16


def split(x):
    hi = x.astype(BF16)
    return hi, (x - hi.astype(F32)).astype(BF16)


def mm(a, b):
    return jnp.dot(a, b, preferred_element_type=F32)


def mm_nt(a, b):
    return lax.dot_general(a, b, (((1,), (1,)), ((), ())), preferred_element_type=F32)


def pack_left(a):
    hi, lo = split(a)
    return jnp.concatenate([hi, lo], axis=1)


def pack_right(b):
    hi, lo = split(b)
    row = jnp.concatenate([hi, lo], axis=1)
    return jnp.concatenate([row, row], axis=0)


def fold(r):
    return r[:, :128] + r[:, 128:]


def mm_small(a, b):
    return fold(mm(pack_left(a), pack_right(b)))


def mm_wide(a, b):
    ah, al = split(a)
    bh, bl = split(b)
    return mm(jnp.concatenate([ah, al], axis=1), jnp.concatenate([bh, bh], axis=0)) + mm(ah, bl)


def decay_rows(gate, live):
    x = jnp.where(live, -(jnp.maximum(gate, 0.0) + jnp.log1p(jnp.exp(-jnp.abs(gate)))), 0.0)
    lane = lax.broadcasted_iota(jnp.int32, x.shape, 1)
    step = 1
    while step < 256:
        x = x + jnp.where(lane >= step, pltpu.roll(x, step, 1), 0.0)
        step *= 2
    return x


def to_columns(rows):
    pad = jnp.zeros((128 - rows.shape[0], 256), F32)
    return jnp.concatenate([rows, pad], axis=0).T


def live_lanes(info_ref):
    edge = info_ref[1] * 128 - info_ref[0] * 256
    return lax.broadcasted_iota(jnp.int32, (8, 256), 1) < edge


def log_norm(x):
    return -0.5 * jnp.log(jnp.sum(x * x, axis=1, keepdims=True) + 1e-06)


def split3(x):
    hi = x.astype(BF16)
    r = x - hi.astype(F32)
    mid = r.astype(BF16)
    lo = (r - mid.astype(F32)).astype(BF16)
    return hi, mid, lo


def mm_tn(a, b):
    return lax.dot_general(a, b, (((0,), (0,)), ((), ())), preferred_element_type=F32)


def twice(pair):
    row = jnp.concatenate(pair, axis=1)
    return jnp.concatenate([row, row], axis=0)


def picked(x, b, odd):
    return jnp.concatenate([x[i : i + b] for i in range(odd * b, 128, 2 * b)], axis=0)


def woven(even, odd, b):
    parts = []
    for i in range(0, 64, b):
        parts += [even[i : i + b], odd[i : i + b]]
    return jnp.concatenate(parts, axis=0)


def log_beta(x):
    return -(jnp.maximum(-x, 0.0) + jnp.log1p(jnp.exp(-jnp.abs(x))))


def spans(left, right):
    ones = jnp.ones((24, 256), F32)
    lhs = jnp.concatenate([p.astype(F32) for p in split3(left)] + [ones, jnp.zeros((80, 256), F32)], axis=0)
    cols = lhs.T.astype(BF16)
    rhs = jnp.concatenate([ones.astype(F32)] + [p.astype(F32) for p in split3(-right)] + [jnp.zeros((80, 256), F32)], axis=0)
    at = lax.broadcasted_iota(jnp.int32, (128, 256), 0) % 8
    return cols, lambda h: jnp.where(at == h, rhs, 0.0).astype(BF16)


def maps_kernel(
    tb_hbm, k_hbm, v_hbm, g_hbm, b_hbm, pay_ref, keep_ref, x_ref, l21,
    tb, kr, vr, gr, br, kf, vf, kks, kt, rows, l11, l22, cmp_ref, xc, sems,
):
    copies = [
        pltpu.make_async_copy(src, dst, sems.at[i])
        for i, (src, dst) in enumerate(
            [(tb_hbm, tb), (k_hbm, kr), (g_hbm, gr), (b_hbm, br), (v_hbm, vr)]
        )
    ]
    for c in copies:
        c.start()
    ctx = lax.axis_index("ctx")
    row = lax.broadcasted_iota(jnp.int32, (128, 128), 0)
    col = lax.broadcasted_iota(jnp.int32, (128, 128), 1)
    lower = row > col
    eye = row == col
    copies[1].wait()
    kf[...] = kr[...].astype(F32)
    norms = []
    for kh in range(4):
        kx = kf[pl.ds(kh, 256, stride=4), :]
        k = kx.astype(BF16)
        kt[kh] = kx.T
        kk1 = mm_nt(k[:128], k[:128])
        kk2 = mm_nt(k[128:], k)
        kks[kh, :128, :128] = kk1
        kks[kh, 128:] = kk2
        s1 = jnp.sum(jnp.where(eye, kk1, 0.0), axis=0, keepdims=True)
        s2 = jnp.sum(jnp.where(eye, kk2[:, 128:], 0.0), axis=0, keepdims=True)
        norms.append(jnp.concatenate([s1, s2], axis=1))
    ln = -0.5 * jnp.log(jnp.concatenate([norms[h // 2] for h in range(8)], axis=0) + 1e-06)
    copies[0].wait()
    copies[2].wait()
    copies[3].wait()
    edge = tb[0] * 128 - ctx * 256
    live = lax.broadcasted_iota(jnp.int32, (8, 256), 1) < edge
    G = decay_rows(gr[...], live)
    a = G + ln + jnp.where(live, log_beta(br[...]), -1e4)
    last = G[:, 255:256]
    rows[0] = jnp.exp(a)
    rows[1] = jnp.where(live, jnp.exp(log_beta(br[...])), 0.0)
    rows[2] = jnp.exp(last - G + ln)
    rows[3] = jnp.broadcast_to(jnp.exp(last), (8, 256))
    cols, right = spans(a, G - ln)
    for h in range(8):
        kh = h // 2
        r = right(h)
        d1 = mm(cols[:128], r[:, :128])
        d2 = mm(cols[128:], r)
        l11[h] = jnp.where(lower, jnp.exp(d1) * kks[kh, :128, :128], 0.0)
        l21[h] = jnp.exp(d2[:, :128]) * kks[kh, 128:, :128]
        l22[h] = jnp.where(lower, jnp.exp(d2[:, 128:]) * kks[kh, 128:, 128:], 0.0)

    group = lax.broadcasted_iota(jnp.int32, (16, 128), 1) // 16
    for kb in range(16):
        src = l11 if kb < 8 else l22
        r0 = (kb % 8) * 16
        acc = jnp.zeros((16, 128), F32)
        for q in range(8):
            t = src[q, r0 : r0 + 16, :]
            shift = (q * 16 - r0) % 128
            if shift:
                t = pltpu.roll(t, shift, 1)
            acc = jnp.where(group == q, t, acc)
        cmp_ref[kb * 16 : kb * 16 + 16, :] = acc

    lane = lax.broadcasted_iota(jnp.int32, (16, 128), 1)
    base = (lane // 16) * 16
    xs = [jnp.where(lane % 16 == i, 1.0, 0.0).astype(F32) for i in range(16)]
    ls = [cmp_ref[pl.ds(i, 16, stride=16), :] for i in range(16)]
    for j in range(16):
        xc[pl.ds(j, 16, stride=16), :] = xs[j]
        for i in range(j + 1, 16):
            coef = jnp.take_along_axis(ls[i], base + j, axis=1, mode="promise_in_bounds")
            xs[i] = xs[i] - coef * xs[j]

    block = row // 16 == col // 16
    for h in range(8):
        for part, src in ((0, l11), (1, l22)):
            x = xc[part * 128 : part * 128 + 128, :]
            x = jnp.take_along_axis(x, h * 16 + col % 16, axis=1, mode="promise_in_bounds")
            x_ref[h, part] = jnp.where(block, x, 0.0)
    halfrow = lax.broadcasted_iota(jnp.int32, (64, 128), 0)
    halfcol = lax.broadcasted_iota(jnp.int32, (64, 128), 1)
    for b in (16, 32, 64):
        under = halfcol // b == (halfrow // b) * 2
        for h in range(8):
            for part, src in ((0, l11), (1, l22)):
                x = x_ref[h, part]
                l = jnp.where(under, picked(src[h], b, 1), 0.0)
                m = fold(mm(pack_left(l), pack_right(x)))
                zero = jnp.zeros((64, 128), BF16)
                mh, ml = split(m)
                odd = picked(x, b, 1)
                right_m = twice([woven(zero, mh, b), woven(zero, ml, b)])
                odd = odd - fold(mm(pack_left(odd), right_m))
                x_ref[h, part] = woven(picked(x, b, 0), odd, b)

    copies[4].wait()
    vf[...] = vr[...].astype(F32)
    for h in range(8):
        kh = h // 2
        k = kf[pl.ds(kh, 256, stride=4), :].astype(BF16)
        v = vf[pl.ds(h, 256, stride=8), :].astype(BF16)
        ktz = kt[kh] * rows[2, h : h + 1, :]
        b2 = mm_small(ktz[:, 128:], x_ref[h, 1])
        b1 = mm_small(ktz[:, :128] - mm_small(b2, l21[h]), x_ref[h, 0])
        bb = jnp.concatenate([b1, b2], axis=1)
        t = mm(jnp.concatenate(split(bb * rows[0, h : h + 1, :]), axis=0), k)
        u = mm(jnp.concatenate(split(bb * rows[1, h : h + 1, :]), axis=0), v)
        t = jnp.where(eye, rows[3, h : h + 1, :128], 0.0) - (t[:128] + t[128:])
        u = u[:128] + u[128:]
        pay_ref[h] = jnp.where(ctx == 0, u, jnp.concatenate([t[:64], u[:64]], axis=0))
        keep_ref[h] = jnp.concatenate([t[64:], u[64:]], axis=0)


HEADS_PER_STEP = 4


def vm():
    return pl.BlockSpec(memory_space=pltpu.VMEM)


def sm():
    return pl.BlockSpec(memory_space=pltpu.SMEM)


def hbm():
    return pl.BlockSpec(memory_space=pltpu.HBM)


VL = 60


def maps(tb, k, v, g, b):
    big = lambda *s: pltpu.VMEM(s, F32)
    return pl.pallas_call(
        maps_kernel,
        out_shape=[
            jax.ShapeDtypeStruct((8, 128, 128), F32),
            jax.ShapeDtypeStruct((8, 128, 128), F32),
            jax.ShapeDtypeStruct((8, 2, 128, 128), F32),
            jax.ShapeDtypeStruct((8, 128, 128), F32),
        ],
        in_specs=[hbm()] * 5,
        out_specs=[vm()] * 4,
        scratch_shapes=[
            pltpu.SMEM((1,), jnp.int32),
            pltpu.VMEM((1024, 128), BF16), pltpu.VMEM((2048, 128), BF16), big(8, 256), big(8, 256),
            big(1024, 128), big(2048, 128), big(4, 256, 256), big(4, 128, 256), big(4, 8, 256),
            big(8, 128, 128), big(8, 128, 128),
            big(256, 128), big(256, 128),
            pltpu.SemaphoreType.DMA((5,)),
        ],
        compiler_params=pltpu.CompilerParams(vmem_limit_bytes=VL * 2**20),
        name="maps",
    )(tb, k, v, g, b)


def final_kernel(pay_ref, keep_ref, got_ref, out_ref):
    def work(a_ref, m_ref):
        for h in range(8):
            out_ref[pl.ds(h * 64, 64), :] = mm_small(a_ref[h, :64], m_ref[h]) + a_ref[h, 64:]

    first = lax.axis_index("ctx") == 0

    @pl.when(first)
    def _():
        work(got_ref, pay_ref)

    @pl.when(jnp.logical_not(first))
    def _():
        work(keep_ref, got_ref)


def final(pay, keep, got):
    return pl.pallas_call(
        final_kernel,
        out_shape=jax.ShapeDtypeStruct((512, 128), F32),
        in_specs=[vm(), vm(), vm()],
        out_specs=vm(),
        compiler_params=pltpu.CompilerParams(vmem_limit_bytes=32 * 2**20),
        name="final",
    )(pay, keep, got)


def reads_kernel(tb, q_ref, k_ref, v_ref, g_ref, b_ref, x_ref, l_ref, m_ref, o_ref, qf, kf, vf, rcol, bcol, ecol, of):
    qf[...] = q_ref[...].astype(F32)
    kf[...] = k_ref[...].astype(F32)
    vf[...] = v_ref[...].astype(F32)
    ctx = lax.axis_index("ctx")
    edge = tb[0] * 128 - ctx * 256
    live = lax.broadcasted_iota(jnp.int32, (8, 256), 1) < edge
    G = decay_rows(g_ref[...], live)
    lb = log_beta(b_ref[...])
    lane = lax.broadcasted_iota(jnp.int32, (256, 128), 1)
    norms = jnp.zeros((256, 128), F32)
    for kh in range(4):
        nk = log_norm(kf[pl.ds(kh, 256, stride=4), :])
        nq = log_norm(qf[pl.ds(kh, 256, stride=4), :])
        for h in (2 * kh, 2 * kh + 1):
            norms = jnp.where(lane == h, nk, norms)
            norms = jnp.where(lane == 8 + h, nq, norms)
    norm_rows = norms.T
    nk, nq = norm_rows[:8], norm_rows[8:16]
    p = G + nq
    a = G + nk + jnp.where(live, lb, -1e4)
    scale = to_columns(jnp.concatenate([jnp.exp(a), jnp.where(live, jnp.exp(lb), 0.0), jnp.exp(p)], axis=0))
    for h in range(8):
        rcol[h] = jnp.broadcast_to(scale[:, h : h + 1], (256, 128))
        bcol[h] = jnp.broadcast_to(scale[:, 8 + h : 9 + h], (256, 128))
        ecol[h] = jnp.broadcast_to(scale[:, 16 + h : 17 + h], (256, 128))
    cols, right = spans(p, G - nk)
    row = lax.broadcasted_iota(jnp.int32, (128, 128), 0)
    col = lax.broadcasted_iota(jnp.int32, (128, 128), 1)
    lower = row >= col
    has = (ctx != 0).astype(F32)
    live1, live2 = edge > 0, edge > 128
    for kh in range(4):
        k = kf[pl.ds(kh, 256, stride=4), :].astype(BF16)
        q = qf[pl.ds(kh, 256, stride=4), :].astype(BF16)
        qk1 = mm_nt(q[:128], k[:128])
        qk2 = mm_nt(q[128:], k)
        kq = jnp.concatenate([k, q], axis=0)
        for h in (2 * kh, 2 * kh + 1):
            mrow = jnp.concatenate(split(m_ref[h] * has), axis=1)
            km = fold(mm(kq, mrow))
            d = bcol[h] * vf[pl.ds(h, 256, stride=8), :] - rcol[h] * km[:256]
            d1 = mm_small(x_ref[h, 0], d[:128])
            d2 = mm_small(x_ref[h, 1], d[128:] - mm_small(l_ref[h], d1))
            qm = km[256:] * ecol[h]
            r = right(h)
            e1 = mm(cols[:128], r[:, :128])
            e2 = mm(cols[128:], r)
            p11 = jnp.where(lower, jnp.exp(e1) * qk1, 0.0)
            p21 = jnp.exp(e2[:, :128]) * qk2[:, :128]
            p22 = jnp.where(lower, jnp.exp(e2[:, 128:]) * qk2[:, 128:], 0.0)
            o1 = qm[:128] + mm_small(p11, d1)
            ph, pl_ = split(jnp.concatenate([p21, p22], axis=1))
            dh, dl = split(jnp.concatenate([d1, d2], axis=0))
            o2 = qm[128:] + fold(mm(ph, jnp.concatenate([dh, dl], axis=1))) + mm(pl_, dh)
            o1 = jnp.where(live1, o1, 0.0)
            o2 = jnp.where(live2, o2, 0.0)
            of[pl.ds(h, 256, stride=8), :] = jnp.concatenate([o1, o2], axis=0)
    o_ref[...] = of[...].astype(BF16)


def reads(tb, q, k, v, g, b, x, l, m):
    big = lambda *s: pltpu.VMEM(s, F32)
    return pl.pallas_call(
        reads_kernel,
        out_shape=jax.ShapeDtypeStruct((2048, 128), BF16),
        in_specs=[sm()] + [vm()] * 8,
        out_specs=vm(),
        scratch_shapes=[
            big(1024, 128), big(1024, 128), big(2048, 128),
            big(8, 256, 128), big(8, 256, 128), big(8, 256, 128), big(2048, 128),
        ],
        compiler_params=pltpu.CompilerParams(vmem_limit_bytes=40 * 2**20),
        cost_estimate=pl.CostEstimate(flops=8 * 4 * 2 * 256**3, bytes_accessed=4 * 2**20, transcendentals=0),
        name="reads",
    )(tb, q, k, v, g, b, x, l, m)


def local(queries, keys, values, gate_logit, beta_logit, token_blocks, slot_map):
    q = queries.reshape(1024, 128)
    k = keys.reshape(1024, 128)
    v = values.reshape(2048, 128)
    g = gate_logit.reshape(8, 256)
    b = beta_logit.reshape(8, 256)
    pay, keep, x, l = maps(token_blocks, k, v, g, b)
    got = lax.ppermute(pay, "ctx", [(0, 1), (1, 0)])
    rows = final(pay, keep, got)
    spread = lax.all_to_all(rows.reshape(32, 16, 128), "sess", 0, 0, tiled=True)
    out = reads(token_blocks, q, k, v, g, b, x, l, got)
    place = jnp.arange(32, dtype=jnp.int32)
    owner = jnp.sum(jnp.where(slot_map[None, :] == place[:, None], place[None, :], 0), axis=1)
    back = lax.all_to_all(jnp.take(spread, owner, axis=0, mode="clip"), "sess", 0, 0, tiled=True)
    return out.reshape(1, 256, 8, 128), back.reshape(1, 8, 64, 128)


def solution(mesh):
    from jax.sharding import PartitionSpec as P
    placed = (
        P("sess", "ctx", "head", None), P("sess", "ctx", "head", None), P("sess", "ctx", "head", None),
        P("sess", "head", "ctx"), P("sess", "head", "ctx"), P("sess"), P(),
    )
    return jax.shard_map(
        local, mesh=mesh, in_specs=placed,
        out_specs=(P("sess", "ctx", "head", None), P("sess", "head", "ctx", None)),
        check_vma=False,
    )
```

```python
import functools
import jax
import jax.numpy as jnp
from jax import lax
from jax.experimental import pallas as pl
from jax.experimental.pallas import tpu as pltpu

F32 = jnp.float32
BF16 = jnp.bfloat16


def split(x):
    hi = x.astype(BF16)
    return hi, (x - hi.astype(F32)).astype(BF16)


def mm(a, b):
    return jnp.dot(a, b, preferred_element_type=F32)


def mm_nt(a, b):
    return lax.dot_general(a, b, (((1,), (1,)), ((), ())), preferred_element_type=F32)


def pack_left(a):
    hi, lo = split(a)
    return jnp.concatenate([hi, lo], axis=1)


def pack_right(b):
    hi, lo = split(b)
    row = jnp.concatenate([hi, lo], axis=1)
    return jnp.concatenate([row, row], axis=0)


def fold(r):
    return r[:, :128] + r[:, 128:]


def mm_small(a, b):
    return fold(mm(pack_left(a), pack_right(b)))


def mm_wide(a, b):
    ah, al = split(a)
    bh, bl = split(b)
    return mm(jnp.concatenate([ah, al], axis=1), jnp.concatenate([bh, bh], axis=0)) + mm(ah, bl)


def decay_rows(gate, live):
    x = jnp.where(live, -(jnp.maximum(gate, 0.0) + jnp.log1p(jnp.exp(-jnp.abs(gate)))), 0.0)
    lane = lax.broadcasted_iota(jnp.int32, x.shape, 1)
    step = 1
    while step < 256:
        x = x + jnp.where(lane >= step, pltpu.roll(x, step, 1), 0.0)
        step *= 2
    return x


def to_columns(rows):
    pad = jnp.zeros((128 - rows.shape[0], 256), F32)
    return jnp.concatenate([rows, pad], axis=0).T


def live_lanes(info_ref):
    edge = info_ref[1] * 128 - info_ref[0] * 256
    return lax.broadcasted_iota(jnp.int32, (8, 256), 1) < edge


def log_norm(x):
    return -0.5 * jnp.log(jnp.sum(x * x, axis=1, keepdims=True) + 1e-06)


def split3(x):
    hi = x.astype(BF16)
    r = x - hi.astype(F32)
    mid = r.astype(BF16)
    lo = (r - mid.astype(F32)).astype(BF16)
    return hi, mid, lo


def mm_tn(a, b):
    return lax.dot_general(a, b, (((0,), (0,)), ((), ())), preferred_element_type=F32)


def twice(pair):
    row = jnp.concatenate(pair, axis=1)
    return jnp.concatenate([row, row], axis=0)


def picked(x, b, odd):
    return jnp.concatenate([x[i : i + b] for i in range(odd * b, 128, 2 * b)], axis=0)


def woven(even, odd, b):
    parts = []
    for i in range(0, 64, b):
        parts += [even[i : i + b], odd[i : i + b]]
    return jnp.concatenate(parts, axis=0)


def log_beta(x):
    return -(jnp.maximum(-x, 0.0) + jnp.log1p(jnp.exp(-jnp.abs(x))))


def prod(left, right):
    if MODE == 0:
        return fold(mm(left, jnp.concatenate([right, right], axis=0)))
    m = left.shape[0]
    r = mm(jnp.concatenate([left[:, :128], left[:, 128:]], axis=0), right)
    return r[:m, :128] + r[:m, 128:] + r[m:, :128]


def unpack(p):
    return p[:, :128].astype(F32) + p[:, 128:].astype(F32)


def running_sum(x):
    r = lax.broadcasted_iota(jnp.int32, (256, 256), 0)
    c = lax.broadcasted_iota(jnp.int32, (256, 256), 1)
    tri = jnp.where(r <= c, 1.0, 0.0).astype(BF16)
    parts = jnp.concatenate([p.astype(F32) for p in split3(x)] + [jnp.zeros((8, 256), F32)], axis=0)
    y = mm(parts.astype(BF16), tri)
    return y[:8] + y[8:16] + y[16:24]


def spans(left, right):
    ones = jnp.ones((24, 256), F32)
    lhs = jnp.concatenate([p.astype(F32) for p in split3(left)] + [ones, jnp.zeros((80, 256), F32)], axis=0)
    cols = lhs.T.astype(BF16)[:, :64]
    rhs = jnp.concatenate([ones] + [p.astype(F32) for p in split3(-right)] + [jnp.zeros((16, 256), F32)], axis=0)
    at = lax.broadcasted_iota(jnp.int32, (64, 256), 0) % 8
    return cols, lambda h: jnp.where(at == h, rhs, 0.0).astype(BF16)


def maps_kernel(
    tb, slot_hbm, k_hbm, v_hbm, g_hbm, b_hbm, pay_ref, keep_ref, x_ref, l21, slot_ref,
    kr, vr, gr, br, kf, vf, kks, kt, rows, l11, l22, p11, p22, cmp_ref, xc, bb, mid, sems,
):
    copies = [
        pltpu.make_async_copy(src, dst, sems.at[i])
        for i, (src, dst) in enumerate([(k_hbm, kr), (g_hbm, gr), (b_hbm, br), (v_hbm, vr), (slot_hbm, slot_ref)])
    ]
    for c in copies:
        c.start()
    ctx = lax.axis_index("ctx")
    row = lax.broadcasted_iota(jnp.int32, (128, 128), 0)
    col = lax.broadcasted_iota(jnp.int32, (128, 128), 1)
    lower = row > col
    eye = row == col
    copies[1].wait()
    copies[2].wait()
    edge = tb[0] * 128 - ctx * 256
    live = lax.broadcasted_iota(jnp.int32, (8, 256), 1) < edge
    gate = gr[...]
    steps = -(jnp.maximum(gate, 0.0) + jnp.log1p(jnp.exp(-jnp.abs(gate))))
    G = running_sum(jnp.where(live, steps, 0.0))
    lb = log_beta(br[...])
    last = G[:, 255:256]
    rows[1] = jnp.where(live, jnp.exp(lb), 0.0)
    rows[3] = jnp.broadcast_to(jnp.exp(last), (8, 256))
    early = G + jnp.where(live, lb, -1e4)
    copies[0].wait()
    kf[...] = kr[...].astype(F32)
    norms = []
    for kh in range(4):
        kx = kf[pl.ds(kh, 256, stride=4), :]
        k = kx.astype(BF16)
        kt[kh] = kx.T
        kk1 = mm_nt(k[:128], k[:128])
        kk2 = mm_nt(k[128:], k)
        kks[kh, :128, :128] = kk1
        kks[kh, 128:] = kk2
        s1 = jnp.sum(jnp.where(eye, kk1, 0.0), axis=0, keepdims=True)
        s2 = jnp.sum(jnp.where(eye, kk2[:, 128:], 0.0), axis=0, keepdims=True)
        norms.append(jnp.concatenate([s1, s2], axis=1))
    ln = -0.5 * jnp.log(jnp.concatenate([norms[h // 2] for h in range(8)], axis=0) + 1e-06)
    a = early + ln
    rows[0] = jnp.exp(a)
    rows[2] = jnp.exp(last - G + ln)
    cols, right = spans(a, G - ln)
    for h in range(8):
        kh = h // 2
        r = right(h)
        d1 = mm(cols[:128], r[:, :128])
        d2 = mm(cols[128:], r)
        t11 = jnp.where(lower, jnp.exp(d1) * kks[kh, :128, :128], 0.0)
        t22 = jnp.where(lower, jnp.exp(d2[:, 128:]) * kks[kh, 128:, 128:], 0.0)
        l11[h] = t11
        l22[h] = t22
        p11[h] = pack_left(t11)
        p22[h] = pack_left(t22)
        l21[h] = pack_left(jnp.exp(d2[:, :128]) * kks[kh, 128:, :128])

    group = lax.broadcasted_iota(jnp.int32, (16, 128), 1) // 16
    for kb in range(16):
        src = l11 if kb < 8 else l22
        r0 = (kb % 8) * 16
        acc = jnp.zeros((16, 128), F32)
        for q in range(8):
            t = src[q, r0 : r0 + 16, :]
            shift = (q * 16 - r0) % 128
            if shift:
                t = pltpu.roll(t, shift, 1)
            acc = jnp.where(group == q, t, acc)
        cmp_ref[kb * 16 : kb * 16 + 16, :] = acc

    copies[3].wait()
    copies[4].wait()
    vf[...] = vr[...].astype(F32)
    lane = lax.broadcasted_iota(jnp.int32, (16, 128), 1)
    base = (lane // 16) * 16
    xs = [jnp.where(lane % 16 == i, 1.0, 0.0).astype(F32) for i in range(16)]
    ls = [cmp_ref[pl.ds(i, 16, stride=16), :] for i in range(16)]
    for j in range(16):
        xc[pl.ds(j, 16, stride=16), :] = xs[j]
        for i in range(j + 1, 16):
            coef = jnp.take_along_axis(ls[i], base + j, axis=1, mode="promise_in_bounds")
            xs[i] = xs[i] - coef * xs[j]

    block = row // 16 == col // 16
    if EXPAND == 0:
        col16, block16 = col[:EG] % 16, [row[i : i + EG] // 16 == col[i : i + EG] // 16 for i in range(0, 128, EG)]
        for part in range(2):
            for i in range(0, 128, EG):
                x = xc[part * 128 + i : part * 128 + i + EG, :]
                ys = [jnp.take_along_axis(x, h * 16 + col16, axis=1, mode="promise_in_bounds") for h in range(8)]
                ys = [pack_left(jnp.where(block16[i // EG], y, 0.0)) for y in ys]
                for h in range(8):
                    x_ref[h, part, i : i + EG] = ys[h]
    else:
        src = lax.broadcasted_iota(jnp.int32, (128, 256), 0)
        dst = lax.broadcasted_iota(jnp.int32, (128, 256), 1)
        both = jnp.concatenate(split(xc[...]), axis=0)
        for p in range(4):
            pick = jnp.where(src == (2 * p + dst // 128) * 16 + dst % 16, 1.0, 0.0).astype(BF16)
            r = mm(both, pick)
            for s in range(2):
                for part in range(2):
                    hi = jnp.where(block, r[part * 128 : part * 128 + 128, s * 128 : s * 128 + 128], 0.0)
                    lo = jnp.where(block, r[256 + part * 128 : 384 + part * 128, s * 128 : s * 128 + 128], 0.0)
                    x_ref[2 * p + s, part, :, :128] = hi.astype(BF16)
                    x_ref[2 * p + s, part, :, 128:] = lo.astype(BF16)
    halfrow = lax.broadcasted_iota(jnp.int32, (64, 256), 0)
    halfcol = lax.broadcasted_iota(jnp.int32, (64, 256), 1) % 128
    zero = jnp.zeros((64, 256), BF16)
    for b in (16, 32, 64):
        under = halfcol // b == (halfrow // b) * 2
        pairs = [(h, part, src) for h in range(8) for part, src in ((0, p11), (1, p22))]
        for h, part, src in pairs:
            l = jnp.where(under, picked(src[h], b, 1), zero)
            mid[h, part] = pack_left(prod(l, x_ref[h, part]))
        for h, part, src in pairs:
            odd = picked(x_ref[h, part], b, 1)
            new = pack_left(unpack(odd) - prod(odd, woven(zero, mid[h, part], b)))
            for i in range(0, 64, b):
                x_ref[h, part, 2 * i + b : 2 * i + 2 * b] = new[i : i + b]

    for h in range(8):
        ktz = kt[h // 2] * rows[2, h : h + 1, :]
        b2 = prod(pack_left(ktz[:, 128:]), x_ref[h, 1])
        bb[h, :, 128:] = b2
        l11[h] = ktz[:, :128]
        p22[h] = pack_left(b2)
    for h in range(8):
        p11[h] = pack_left(l11[h] - prod(p22[h], l21[h]))
    for h in range(8):
        bb[h, :, :128] = prod(p11[h], x_ref[h, 0])
    for h in range(8):
        k = kf[pl.ds((h // 2), 256, stride=4), :].astype(BF16)
        t = mm(jnp.concatenate(split(bb[h] * rows[0, h : h + 1, :]), axis=0), k)
        t = jnp.where(eye, rows[3, h : h + 1, :128], 0.0) - (t[:128] + t[128:])
        l11[h] = t
        keep_ref[h, :64] = t[64:]
    for h in range(8):
        v = vf[pl.ds(h, 256, stride=8), :].astype(BF16)
        u = mm(jnp.concatenate(split(bb[h] * rows[1, h : h + 1, :]), axis=0), v)
        u = u[:128] + u[128:]
        keep_ref[h, 64:] = u[64:]
        pay_ref[h] = jnp.where(ctx == 0, u, jnp.concatenate([l11[h, :64], u[:64]], axis=0))


HEADS_PER_STEP = 4


def vm():
    return pl.BlockSpec(memory_space=pltpu.VMEM)


def sm():
    return pl.BlockSpec(memory_space=pltpu.SMEM)


def hbm():
    return pl.BlockSpec(memory_space=pltpu.HBM)


VL = 24
MODE = 0
EG = 16
EXPAND = 0


def maps(tb, slot_map, k, v, g, b):
    big = lambda *s: pltpu.VMEM(s, F32)
    return pl.pallas_call(
        maps_kernel,
        out_shape=[
            pltpu.VMEM((8, 128, 128), F32),
            pltpu.VMEM((8, 128, 128), F32),
            pltpu.VMEM((8, 2, 128, 256), BF16),
            pltpu.VMEM((8, 128, 256), BF16),
            pltpu.SMEM((32,), jnp.int32),
        ],
        in_specs=[sm()] + [hbm()] * 5,
        out_specs=[vm()] * 4 + [sm()],
        scratch_shapes=[
            pltpu.VMEM((1024, 128), BF16), pltpu.VMEM((2048, 128), BF16), big(8, 256), big(8, 256),
            big(1024, 128), big(2048, 128), big(4, 256, 256), big(4, 128, 256), big(4, 8, 256),
            big(8, 128, 128), big(8, 128, 128),
            pltpu.VMEM((8, 128, 256), BF16), pltpu.VMEM((8, 128, 256), BF16),
            big(256, 128), big(256, 128), big(8, 128, 256), pltpu.VMEM((8, 2, 64, 256), BF16),
            pltpu.SemaphoreType.DMA((5,)),
        ],
        compiler_params=pltpu.CompilerParams(vmem_limit_bytes=VL * 2**20),
        name="maps",
    )(tb, *[pltpu.with_memory_space_constraint(a, pltpu.HBM) for a in (slot_map, k, v, g, b)])


def final_kernel(pay_ref, keep_ref, got_ref, out_ref):
    def work(a_ref, m_ref):
        for h in range(8):
            out_ref[pl.ds(h * 64, 64), :] = mm_small(a_ref[h, :64], m_ref[h]) + a_ref[h, 64:]

    first = lax.axis_index("ctx") == 0

    @pl.when(first)
    def _():
        work(got_ref, pay_ref)

    @pl.when(jnp.logical_not(first))
    def _():
        work(keep_ref, got_ref)


def final(pay, keep, got):
    return pl.pallas_call(
        final_kernel,
        out_shape=pltpu.VMEM((512, 128), F32),
        in_specs=[vm(), vm(), vm()],
        out_specs=vm(),
        compiler_params=pltpu.CompilerParams(vmem_limit_bytes=16 * 2**20),
        name="final",
    )(pay, keep, got)


def reads_kernel(tb, q_ref, k_ref, v_ref, g_ref, b_ref, x_ref, l_ref, m_ref, o_ref, qf, kf, vf, rcol, bcol, ecol, of):
    qf[...] = q_ref[...].astype(F32)
    kf[...] = k_ref[...].astype(F32)
    vf[...] = v_ref[...].astype(F32)
    ctx = lax.axis_index("ctx")
    edge = tb[0] * 128 - ctx * 256
    live = lax.broadcasted_iota(jnp.int32, (8, 256), 1) < edge
    G = decay_rows(g_ref[...], live)
    lb = log_beta(b_ref[...])
    lane = lax.broadcasted_iota(jnp.int32, (256, 128), 1)
    norms = jnp.zeros((256, 128), F32)
    for kh in range(4):
        nk = log_norm(kf[pl.ds(kh, 256, stride=4), :])
        nq = log_norm(qf[pl.ds(kh, 256, stride=4), :])
        for h in (2 * kh, 2 * kh + 1):
            norms = jnp.where(lane == h, nk, norms)
            norms = jnp.where(lane == 8 + h, nq, norms)
    norm_rows = norms.T
    nk, nq = norm_rows[:8], norm_rows[8:16]
    p = G + nq
    a = G + nk + jnp.where(live, lb, -1e4)
    scale = to_columns(jnp.concatenate([jnp.exp(a), jnp.where(live, jnp.exp(lb), 0.0), jnp.exp(p)], axis=0))
    for h in range(8):
        rcol[h] = jnp.broadcast_to(scale[:, h : h + 1], (256, 128))
        bcol[h] = jnp.broadcast_to(scale[:, 8 + h : 9 + h], (256, 128))
        ecol[h] = jnp.broadcast_to(scale[:, 16 + h : 17 + h], (256, 128))
    cols, right = spans(p, G - nk)
    row = lax.broadcasted_iota(jnp.int32, (128, 128), 0)
    col = lax.broadcasted_iota(jnp.int32, (128, 128), 1)
    lower = row >= col
    has = (ctx != 0).astype(F32)
    live1, live2 = edge > 0, edge > 128
    for kh in range(4):
        k = kf[pl.ds(kh, 256, stride=4), :].astype(BF16)
        q = qf[pl.ds(kh, 256, stride=4), :].astype(BF16)
        qk1 = mm_nt(q[:128], k[:128])
        qk2 = mm_nt(q[128:], k)
        kq = jnp.concatenate([k, q], axis=0)
        for h in (2 * kh, 2 * kh + 1):
            mrow = jnp.concatenate(split(m_ref[h] * has), axis=1)
            km = fold(mm(kq, mrow))
            d = bcol[h] * vf[pl.ds(h, 256, stride=8), :] - rcol[h] * km[:256]
            d1 = prod(x_ref[h, 0], pack_left(d[:128]))
            d2 = prod(x_ref[h, 1], pack_left(d[128:] - prod(l_ref[h], pack_left(d1))))
            qm = km[256:] * ecol[h]
            r = right(h)
            e1 = mm(cols[:128], r[:, :128])
            e2 = mm(cols[128:], r)
            p11 = jnp.where(lower, jnp.exp(e1) * qk1, 0.0)
            p21 = jnp.exp(e2[:, :128]) * qk2[:, :128]
            p22 = jnp.where(lower, jnp.exp(e2[:, 128:]) * qk2[:, 128:], 0.0)
            o1 = qm[:128] + mm_small(p11, d1)
            ph, pl_ = split(jnp.concatenate([p21, p22], axis=1))
            dh, dl = split(jnp.concatenate([d1, d2], axis=0))
            o2 = qm[128:] + fold(mm(ph, jnp.concatenate([dh, dl], axis=1))) + mm(pl_, dh)
            o1 = jnp.where(live1, o1, 0.0)
            o2 = jnp.where(live2, o2, 0.0)
            of[pl.ds(h, 256, stride=8), :] = jnp.concatenate([o1, o2], axis=0)
    o_ref[...] = of[...].astype(BF16)


def reads(tb, q, k, v, g, b, x, l, m):
    big = lambda *s: pltpu.VMEM(s, F32)
    return pl.pallas_call(
        reads_kernel,
        out_shape=jax.ShapeDtypeStruct((2048, 128), BF16),
        in_specs=[sm()] + [vm()] * 8,
        out_specs=vm(),
        scratch_shapes=[
            big(1024, 128), big(1024, 128), big(2048, 128),
            big(8, 256, 128), big(8, 256, 128), big(8, 256, 128), big(2048, 128),
        ],
        compiler_params=pltpu.CompilerParams(vmem_limit_bytes=24 * 2**20),
        cost_estimate=pl.CostEstimate(flops=8 * 4 * 2 * 256**3, bytes_accessed=4 * 2**20, transcendentals=0),
        name="reads",
    )(tb, q, k, v, g, b, x, l, m)


def reorder_kernel(slot_ref, in_ref, out_ref):
    for s in range(32):
        out_ref[slot_ref[s]] = in_ref[s]


def reorder(slot_map, x):
    return pl.pallas_call(
        reorder_kernel,
        out_shape=pltpu.VMEM(x.shape, x.dtype),
        in_specs=[sm(), vm()],
        out_specs=vm(),
        name="reorder",
    )(
        pltpu.with_memory_space_constraint(slot_map, pltpu.SMEM),
        pltpu.with_memory_space_constraint(x, pltpu.VMEM),
    )


def place_kernel(in_ref, out_hbm, sem):
    copy = pltpu.make_async_copy(in_ref, out_hbm, sem)
    copy.start()
    copy.wait()


def place(x):
    return pl.pallas_call(
        place_kernel,
        out_shape=jax.ShapeDtypeStruct(x.shape, x.dtype),
        in_specs=[vm()],
        out_specs=hbm(),
        scratch_shapes=[pltpu.SemaphoreType.DMA],
        name="place",
    )(pltpu.with_memory_space_constraint(x, pltpu.VMEM))


def local(queries, keys, values, gate_logit, beta_logit, token_blocks, slot_map):
    q = queries.reshape(1024, 128)
    k = keys.reshape(1024, 128)
    v = values.reshape(2048, 128)
    g = gate_logit.reshape(8, 256)
    b = beta_logit.reshape(8, 256)
    pay, keep, x, l, slots = maps(token_blocks, slot_map, k, v, g, b)
    got = lax.ppermute(pay, "ctx", [(0, 1), (1, 0)])
    rows = final(pay, keep, got)
    spread = lax.all_to_all(rows.reshape(32, 16, 128), "sess", 0, 0, tiled=True)
    out = reads(token_blocks, q, k, v, g, b, x, l, got)
    back = lax.all_to_all(reorder(slots, spread), "sess", 0, 0, tiled=True)
    back = place(back.reshape(1, 8, 64, 128))
    return out.reshape(1, 256, 8, 128), back


def solution(mesh):
    from jax.sharding import PartitionSpec as P
    placed = (
        P("sess", "ctx", "head", None), P("sess", "ctx", "head", None), P("sess", "ctx", "head", None),
        P("sess", "head", "ctx"), P("sess", "head", "ctx"), P("sess"), P(),
    )
    return jax.shard_map(
        local, mesh=mesh, in_specs=placed,
        out_specs=(P("sess", "ctx", "head", None), P("sess", "head", "ctx", None)),
        check_vma=False,
    )
```

```python
import functools
import jax
import jax.numpy as jnp
from jax import lax
from jax.experimental import pallas as pl
from jax.experimental.pallas import tpu as pltpu

F32 = jnp.float32
BF16 = jnp.bfloat16


def split(x):
    hi = x.astype(BF16)
    return hi, (x - hi.astype(F32)).astype(BF16)


def mm(a, b):
    return jnp.dot(a, b, preferred_element_type=F32)


def mm_nt(a, b):
    return lax.dot_general(a, b, (((1,), (1,)), ((), ())), preferred_element_type=F32)


def pack_left(a):
    hi, lo = split(a)
    return jnp.concatenate([hi, lo], axis=1)


def pack_right(b):
    hi, lo = split(b)
    row = jnp.concatenate([hi, lo], axis=1)
    return jnp.concatenate([row, row], axis=0)


def fold(r):
    return r[:, :128] + r[:, 128:]


def mm_small(a, b):
    return fold(mm(pack_left(a), pack_right(b)))


def decay_rows(gate, live):
    x = jnp.where(live, -(jnp.maximum(gate, 0.0) + jnp.log1p(jnp.exp(-jnp.abs(gate)))), 0.0)
    lane = lax.broadcasted_iota(jnp.int32, x.shape, 1)
    step = 1
    while step < 256:
        x = x + jnp.where(lane >= step, pltpu.roll(x, step, 1), 0.0)
        step *= 2
    return x


def to_columns(rows):
    pad = jnp.zeros((128 - rows.shape[0], 256), F32)
    return jnp.concatenate([rows, pad], axis=0).T


def live_lanes(info_ref):
    edge = info_ref[1] * 128 - info_ref[0] * 256
    return lax.broadcasted_iota(jnp.int32, (8, 256), 1) < edge


def log_norm(x):
    return -0.5 * jnp.log(jnp.sum(x * x, axis=1, keepdims=True) + 1e-06)


def split3(x):
    hi = x.astype(BF16)
    r = x - hi.astype(F32)
    mid = r.astype(BF16)
    lo = (r - mid.astype(F32)).astype(BF16)
    return hi, mid, lo


def picked(x, b, odd):
    return jnp.concatenate([x[i : i + b] for i in range(odd * b, 128, 2 * b)], axis=0)


def rows_of(ref, at, b, odd):
    return jnp.concatenate([ref[at + (slice(i, i + b),)] for i in range(odd * b, 128, 2 * b)], axis=0)


def woven(even, odd, b):
    parts = []
    for i in range(0, 64, b):
        parts += [even[i : i + b], odd[i : i + b]]
    return jnp.concatenate(parts, axis=0)


def log_beta(x):
    return -(jnp.maximum(-x, 0.0) + jnp.log1p(jnp.exp(-jnp.abs(x))))


def prod(left, right):
    return fold(mm(left, jnp.concatenate([right, right], axis=0)))


def unpack(p):
    return p[:, :128].astype(F32) + p[:, 128:].astype(F32)


def running_sum(x):
    r = lax.broadcasted_iota(jnp.int32, (256, 256), 0)
    c = lax.broadcasted_iota(jnp.int32, (256, 256), 1)
    tri = jnp.where(r <= c, 1.0, 0.0).astype(BF16)
    parts = jnp.concatenate([p.astype(F32) for p in split3(x)] + [jnp.zeros((8, 256), F32)], axis=0)
    y = mm(parts.astype(BF16), tri)
    return y[:8] + y[8:16] + y[16:24]


def spans(left, right):
    ones = jnp.ones((24, 256), F32)
    lhs = jnp.concatenate([p.astype(F32) for p in split3(left)] + [ones, jnp.zeros((80, 256), F32)], axis=0)
    cols = lhs.T.astype(BF16)[:, :64]
    rhs = jnp.concatenate([ones] + [p.astype(F32) for p in split3(-right)] + [jnp.zeros((16, 256), F32)], axis=0)
    at = lax.broadcasted_iota(jnp.int32, (64, 256), 0) % 8
    return cols, lambda h: jnp.where(at == h, rhs, 0.0).astype(BF16)


def maps_kernel(
    tb, slot_hbm, k_hbm, v_hbm, g_hbm, b_hbm, pay_ref, keep_ref, x_ref, l21, slot_ref,
    kr, vr, gr, br, kf, vf, kks, kt, rows, l11, l22, p11, p22, cmp_ref, xc, sems,
):
    copies = [
        pltpu.make_async_copy(src, dst, sems.at[i])
        for i, (src, dst) in enumerate([(k_hbm, kr), (g_hbm, gr), (b_hbm, br), (v_hbm, vr), (slot_hbm, slot_ref)])
    ]
    for c in copies:
        c.start()
    ctx = lax.axis_index("ctx")
    row = lax.broadcasted_iota(jnp.int32, (128, 128), 0)
    col = lax.broadcasted_iota(jnp.int32, (128, 128), 1)
    lower = row > col
    eye = row == col
    copies[1].wait()
    copies[2].wait()
    edge = tb[0] * 128 - ctx * 256
    live = lax.broadcasted_iota(jnp.int32, (8, 256), 1) < edge
    gate = gr[...]
    steps = -(jnp.maximum(gate, 0.0) + jnp.log1p(jnp.exp(-jnp.abs(gate))))
    G = running_sum(jnp.where(live, steps, 0.0))
    lb = log_beta(br[...])
    last = G[:, 255:256]
    rows[1] = jnp.where(live, jnp.exp(lb), 0.0)
    rows[3] = jnp.broadcast_to(jnp.exp(last), (8, 256))
    early = G + jnp.where(live, lb, -1e4)
    copies[0].wait()
    kf[...] = kr[...].astype(F32)
    norms = []
    for kh in range(4):
        kx = kf[pl.ds(kh, 256, stride=4), :]
        k = kx.astype(BF16)
        kt[kh] = kx.T
        kk1 = mm_nt(k[:128], k[:128])
        kk2 = mm_nt(k[128:], k)
        kks[kh, :128, :128] = kk1
        kks[kh, 128:] = kk2
        s1 = jnp.sum(jnp.where(eye, kk1, 0.0), axis=0, keepdims=True)
        s2 = jnp.sum(jnp.where(eye, kk2[:, 128:], 0.0), axis=0, keepdims=True)
        norms.append(jnp.concatenate([s1, s2], axis=1))
    ln = -0.5 * jnp.log(jnp.concatenate([norms[h // 2] for h in range(8)], axis=0) + 1e-06)
    a = early + ln
    rows[0] = jnp.exp(a)
    rows[2] = jnp.exp(last - G + ln)
    cols, right = spans(a, G - ln)
    for h in range(8):
        kh = h // 2
        r = right(h)
        d1 = mm(cols[:128], r[:, :128])
        d2 = mm(cols[128:], r)
        t11 = jnp.where(lower, jnp.exp(d1) * kks[kh, :128, :128], 0.0)
        t22 = jnp.where(lower, jnp.exp(d2[:, 128:]) * kks[kh, 128:, 128:], 0.0)
        l11[h] = t11
        l22[h] = t22
        p11[h] = pack_left(t11)
        p22[h] = pack_left(t22)
        l21[h] = pack_left(jnp.exp(d2[:, :128]) * kks[kh, 128:, :128])

    group = lax.broadcasted_iota(jnp.int32, (16, 128), 1) // 16
    for kb in range(16):
        src = l11 if kb < 8 else l22
        r0 = (kb % 8) * 16
        acc = jnp.zeros((16, 128), F32)
        for q in range(8):
            t = src[q, r0 : r0 + 16, :]
            shift = (q * 16 - r0) % 128
            if shift:
                t = pltpu.roll(t, shift, 1)
            acc = jnp.where(group == q, t, acc)
        cmp_ref[kb * 16 : kb * 16 + 16, :] = acc

    copies[3].wait()
    copies[4].wait()
    lane = lax.broadcasted_iota(jnp.int32, (16, 128), 1)
    base = (lane // 16) * 16
    xs = [jnp.where(lane % 16 == i, 1.0, 0.0).astype(F32) for i in range(16)]
    ls = [cmp_ref[pl.ds(i, 16, stride=16), :] for i in range(16)]
    for j in range(16):
        xc[pl.ds(j, 16, stride=16), :] = xs[j]
        vf[j * 128 : j * 128 + 128] = vr[j * 128 : j * 128 + 128].astype(F32)
        for i in range(j + 1, 16):
            coef = jnp.take_along_axis(ls[i], base + j, axis=1, mode="promise_in_bounds")
            xs[i] = xs[i] - coef * xs[j]

    col16 = col[:16] % 16
    block16 = [row[i : i + 16] // 16 == col[i : i + 16] // 16 for i in range(0, 128, 16)]
    halfrow = lax.broadcasted_iota(jnp.int32, (64, 256), 0)
    halfcol = lax.broadcasted_iota(jnp.int32, (64, 256), 1) % 128
    zero = jnp.zeros((64, 256), BF16)
    under = {
        b: jnp.where(halfcol // b == (halfrow // b) * 2, 1.0, 0.0).astype(BF16) for b in (16, 32, 64)
    }

    X, MID, TMP, BB = {}, {}, {}, {}

    def expand(h):
        for part in range(2):
            tiles = []
            for i in range(0, 128, 16):
                x = xc[part * 128 + i : part * 128 + i + 16, :]
                x = jnp.take_along_axis(x, h * 16 + col16, axis=1, mode="promise_in_bounds")
                tiles.append(pack_left(jnp.where(block16[i // 16], x, 0.0)))
            X[h, part] = jnp.concatenate(tiles, axis=0)

    def half_one(b):
        def step(h):
            for part, src in ((0, p11), (1, p22)):
                l = rows_of(src, (h,), b, 1) * under[b]
                MID[h, part] = pack_left(prod(l, X[h, part]))

        return step

    def half_two(b):
        def step(h):
            for part in range(2):
                x = X[h, part]
                odd = picked(x, b, 1)
                new = pack_left(unpack(odd) - prod(odd, woven(zero, MID[h, part], b)))
                X[h, part] = woven(picked(x, b, 0), new, b)
                if b == 64:
                    x_ref[h, part] = X[h, part]

        return step

    def right_half(h):
        ktz = kt[h // 2] * rows[2, h : h + 1, :]
        b2 = prod(pack_left(ktz[:, 128:]), X[h, 1])
        BB[h, 1] = b2
        TMP[h, 0] = ktz[:, :128]
        TMP[h, 1] = pack_left(b2)

    def left_rest(h):
        TMP[h, 2] = pack_left(TMP[h, 0] - prod(TMP[h, 1], l21[h]))

    def left_half(h):
        BB[h, 0] = prod(TMP[h, 2], X[h, 0])

    def to_map(h):
        k = kf[pl.ds((h // 2), 256, stride=4), :].astype(BF16)
        bb = jnp.concatenate([BB[h, 0], BB[h, 1]], axis=1)
        t = mm(jnp.concatenate(split(bb * rows[0, h : h + 1, :]), axis=0), k)
        t = jnp.where(eye, rows[3, h : h + 1, :128], 0.0) - (t[:128] + t[128:])
        TMP[h, 3] = t[:64]
        keep_ref[h, :64] = t[64:]

    def to_state(h):
        v = vf[pl.ds(h, 256, stride=8), :].astype(BF16)
        bb = jnp.concatenate([BB[h, 0], BB[h, 1]], axis=1)
        u = mm(jnp.concatenate(split(bb * rows[1, h : h + 1, :]), axis=0), v)
        u = u[:128] + u[128:]
        keep_ref[h, 64:] = u[64:]
        pay_ref[h] = jnp.where(ctx == 0, u, jnp.concatenate([TMP[h, 3], u[:64]], axis=0))

    steps = [expand]
    for b in (16, 32, 64):
        steps += [half_one(b), half_two(b)]
    steps += [right_half, left_rest, left_half, to_map, to_state]
    for step in steps:
        for h in range(8):
            step(h)


def vm():
    return pl.BlockSpec(memory_space=pltpu.VMEM)


def sm():
    return pl.BlockSpec(memory_space=pltpu.SMEM)


def hbm():
    return pl.BlockSpec(memory_space=pltpu.HBM)


def maps(tb, slot_map, k, v, g, b):
    big = lambda *s: pltpu.VMEM(s, F32)
    return pl.pallas_call(
        maps_kernel,
        out_shape=[
            pltpu.VMEM((8, 128, 128), F32),
            pltpu.VMEM((8, 128, 128), F32),
            pltpu.VMEM((8, 2, 128, 256), BF16),
            pltpu.VMEM((8, 128, 256), BF16),
            pltpu.SMEM((32,), jnp.int32),
        ],
        in_specs=[sm()] + [hbm()] * 5,
        out_specs=[vm()] * 4 + [sm()],
        scratch_shapes=[
            pltpu.VMEM((1024, 128), BF16), pltpu.VMEM((2048, 128), BF16), big(8, 256), big(8, 256),
            big(1024, 128), big(2048, 128), big(4, 256, 256), big(4, 128, 256), big(4, 8, 256),
            big(8, 128, 128), big(8, 128, 128),
            pltpu.VMEM((8, 128, 256), BF16), pltpu.VMEM((8, 128, 256), BF16),
            big(256, 128), big(256, 128),
            pltpu.SemaphoreType.DMA((5,)),
        ],
        compiler_params=pltpu.CompilerParams(vmem_limit_bytes=24 * 2**20),
        name="maps",
    )(tb, *[pltpu.with_memory_space_constraint(a, pltpu.HBM) for a in (slot_map, k, v, g, b)])


def final_kernel(pay_ref, keep_ref, got_ref, out_ref):
    def work(a_ref, m_ref):
        for h in range(8):
            out_ref[pl.ds(h * 64, 64), :] = mm_small(a_ref[h, :64], m_ref[h]) + a_ref[h, 64:]

    first = lax.axis_index("ctx") == 0

    @pl.when(first)
    def _():
        work(got_ref, pay_ref)

    @pl.when(jnp.logical_not(first))
    def _():
        work(keep_ref, got_ref)


def final(pay, keep, got):
    return pl.pallas_call(
        final_kernel,
        out_shape=pltpu.VMEM((512, 128), F32),
        in_specs=[vm(), vm(), vm()],
        out_specs=vm(),
        compiler_params=pltpu.CompilerParams(vmem_limit_bytes=16 * 2**20),
        name="final",
    )(pay, keep, got)


def reads_kernel(tb, q_ref, k_ref, v_ref, g_ref, b_ref, x_ref, l_ref, m_ref, o_ref, qf, kf, vf, rcol, bcol, ecol, of):
    qf[...] = q_ref[...].astype(F32)
    kf[...] = k_ref[...].astype(F32)
    vf[...] = v_ref[...].astype(F32)
    ctx = lax.axis_index("ctx")
    edge = tb[0] * 128 - ctx * 256
    live = lax.broadcasted_iota(jnp.int32, (8, 256), 1) < edge
    G = decay_rows(g_ref[...], live)
    lb = log_beta(b_ref[...])
    lane = lax.broadcasted_iota(jnp.int32, (256, 128), 1)
    norms = jnp.zeros((256, 128), F32)
    for kh in range(4):
        nk = log_norm(kf[pl.ds(kh, 256, stride=4), :])
        nq = log_norm(qf[pl.ds(kh, 256, stride=4), :])
        for h in (2 * kh, 2 * kh + 1):
            norms = jnp.where(lane == h, nk, norms)
            norms = jnp.where(lane == 8 + h, nq, norms)
    norm_rows = norms.T
    nk, nq = norm_rows[:8], norm_rows[8:16]
    p = G + nq
    a = G + nk + jnp.where(live, lb, -1e4)
    scale = to_columns(jnp.concatenate([jnp.exp(a), jnp.where(live, jnp.exp(lb), 0.0), jnp.exp(p)], axis=0))
    for h in range(8):
        rcol[h] = jnp.broadcast_to(scale[:, h : h + 1], (256, 128))
        bcol[h] = jnp.broadcast_to(scale[:, 8 + h : 9 + h], (256, 128))
        ecol[h] = jnp.broadcast_to(scale[:, 16 + h : 17 + h], (256, 128))
    cols, right = spans(p, G - nk)
    row = lax.broadcasted_iota(jnp.int32, (128, 128), 0)
    col = lax.broadcasted_iota(jnp.int32, (128, 128), 1)
    lower = row >= col
    has = (ctx != 0).astype(F32)
    live1, live2 = edge > 0, edge > 128
    for kh in range(4):
        k = kf[pl.ds(kh, 256, stride=4), :].astype(BF16)
        q = qf[pl.ds(kh, 256, stride=4), :].astype(BF16)
        qk1 = mm_nt(q[:128], k[:128])
        qk2 = mm_nt(q[128:], k)
        kq = jnp.concatenate([k, q], axis=0)
        for h in (2 * kh, 2 * kh + 1):
            mrow = jnp.concatenate(split(m_ref[h] * has), axis=1)
            km = fold(mm(kq, mrow))
            d = bcol[h] * vf[pl.ds(h, 256, stride=8), :] - rcol[h] * km[:256]
            d1 = prod(x_ref[h, 0], pack_left(d[:128]))
            d2 = prod(x_ref[h, 1], pack_left(d[128:] - prod(l_ref[h], pack_left(d1))))
            qm = km[256:] * ecol[h]
            r = right(h)
            e1 = mm(cols[:128], r[:, :128])
            e2 = mm(cols[128:], r)
            p11 = jnp.where(lower, jnp.exp(e1) * qk1, 0.0)
            p21 = jnp.exp(e2[:, :128]) * qk2[:, :128]
            p22 = jnp.where(lower, jnp.exp(e2[:, 128:]) * qk2[:, 128:], 0.0)
            o1 = qm[:128] + mm_small(p11, d1)
            ph, pl_ = split(jnp.concatenate([p21, p22], axis=1))
            dh, dl = split(jnp.concatenate([d1, d2], axis=0))
            o2 = qm[128:] + fold(mm(ph, jnp.concatenate([dh, dl], axis=1))) + mm(pl_, dh)
            o1 = jnp.where(live1, o1, 0.0)
            o2 = jnp.where(live2, o2, 0.0)
            of[pl.ds(h, 256, stride=8), :] = jnp.concatenate([o1, o2], axis=0)
    o_ref[...] = of[...].astype(BF16)


def reads(tb, q, k, v, g, b, x, l, m):
    big = lambda *s: pltpu.VMEM(s, F32)
    return pl.pallas_call(
        reads_kernel,
        out_shape=jax.ShapeDtypeStruct((2048, 128), BF16),
        in_specs=[sm()] + [vm()] * 8,
        out_specs=vm(),
        scratch_shapes=[
            big(1024, 128), big(1024, 128), big(2048, 128),
            big(8, 256, 128), big(8, 256, 128), big(8, 256, 128), big(2048, 128),
        ],
        compiler_params=pltpu.CompilerParams(vmem_limit_bytes=24 * 2**20),
        cost_estimate=pl.CostEstimate(flops=8 * 4 * 2 * 256**3, bytes_accessed=4 * 2**20, transcendentals=0),
        name="reads",
    )(tb, q, k, v, g, b, x, l, m)


def reorder_kernel(slot_ref, in_ref, out_ref):
    for s in range(32):
        out_ref[slot_ref[s]] = in_ref[s]


def reorder(slot_map, x):
    return pl.pallas_call(
        reorder_kernel,
        out_shape=pltpu.VMEM(x.shape, x.dtype),
        in_specs=[sm(), vm()],
        out_specs=vm(),
        name="reorder",
    )(
        pltpu.with_memory_space_constraint(slot_map, pltpu.SMEM),
        pltpu.with_memory_space_constraint(x, pltpu.VMEM),
    )


def place_kernel(in_ref, out_hbm, sem):
    copy = pltpu.make_async_copy(in_ref, out_hbm, sem)
    copy.start()
    copy.wait()


def place(x):
    return pl.pallas_call(
        place_kernel,
        out_shape=jax.ShapeDtypeStruct(x.shape, x.dtype),
        in_specs=[vm()],
        out_specs=hbm(),
        scratch_shapes=[pltpu.SemaphoreType.DMA],
        name="place",
    )(pltpu.with_memory_space_constraint(x, pltpu.VMEM))


def local(queries, keys, values, gate_logit, beta_logit, token_blocks, slot_map):
    q = queries.reshape(1024, 128)
    k = keys.reshape(1024, 128)
    v = values.reshape(2048, 128)
    g = gate_logit.reshape(8, 256)
    b = beta_logit.reshape(8, 256)
    pay, keep, x, l, slots = maps(token_blocks, slot_map, k, v, g, b)
    got = lax.ppermute(pay, "ctx", [(0, 1), (1, 0)])
    rows = final(pay, keep, got)
    spread = lax.all_to_all(rows.reshape(32, 16, 128), "sess", 0, 0, tiled=True)
    out = reads(token_blocks, q, k, v, g, b, x, l, got)
    back = lax.all_to_all(reorder(slots, spread), "sess", 0, 0, tiled=True)
    back = place(back.reshape(1, 8, 64, 128))
    return out.reshape(1, 256, 8, 128), back


def solution(mesh):
    from jax.sharding import PartitionSpec as P
    placed = (
        P("sess", "ctx", "head", None), P("sess", "ctx", "head", None), P("sess", "ctx", "head", None),
        P("sess", "head", "ctx"), P("sess", "head", "ctx"), P("sess"), P(),
    )
    return jax.shard_map(
        local, mesh=mesh, in_specs=placed,
        out_specs=(P("sess", "ctx", "head", None), P("sess", "head", "ctx", None)),
        check_vma=False,
    )
```

```python
import functools
import jax
import jax.numpy as jnp
from jax import lax
from jax.experimental import pallas as pl
from jax.experimental.pallas import tpu as pltpu

F32 = jnp.float32
BF16 = jnp.bfloat16


def split(x):
    hi = x.astype(BF16)
    return hi, (x - hi.astype(F32)).astype(BF16)


def mm(a, b):
    return jnp.dot(a, b, preferred_element_type=F32)


def mm_nt(a, b):
    return lax.dot_general(a, b, (((1,), (1,)), ((), ())), preferred_element_type=F32)


def pack_left(a):
    hi, lo = split(a)
    return jnp.concatenate([hi, lo], axis=1)


def pack_right(b):
    hi, lo = split(b)
    row = jnp.concatenate([hi, lo], axis=1)
    return jnp.concatenate([row, row], axis=0)


def fold(r):
    return r[:, :128] + r[:, 128:]


def mm_small(a, b):
    return fold(mm(pack_left(a), pack_right(b)))


def mm_wide(a, b):
    ah, al = split(a)
    bh, bl = split(b)
    return mm(jnp.concatenate([ah, al], axis=1), jnp.concatenate([bh, bh], axis=0)) + mm(ah, bl)


def decay_rows(gate, live):
    x = jnp.where(live, -(jnp.maximum(gate, 0.0) + jnp.log1p(jnp.exp(-jnp.abs(gate)))), 0.0)
    lane = lax.broadcasted_iota(jnp.int32, x.shape, 1)
    step = 1
    while step < 256:
        x = x + jnp.where(lane >= step, pltpu.roll(x, step, 1), 0.0)
        step *= 2
    return x


def to_columns(rows):
    pad = jnp.zeros((128 - rows.shape[0], 256), F32)
    return jnp.concatenate([rows, pad], axis=0).T


def live_lanes(info_ref):
    edge = info_ref[1] * 128 - info_ref[0] * 256
    return lax.broadcasted_iota(jnp.int32, (8, 256), 1) < edge


def log_norm(x):
    return -0.5 * jnp.log(jnp.sum(x * x, axis=1, keepdims=True) + 1e-06)


def split3(x):
    hi = x.astype(BF16)
    r = x - hi.astype(F32)
    mid = r.astype(BF16)
    lo = (r - mid.astype(F32)).astype(BF16)
    return hi, mid, lo


def mm_tn(a, b):
    return lax.dot_general(a, b, (((0,), (0,)), ((), ())), preferred_element_type=F32)


def twice(pair):
    row = jnp.concatenate(pair, axis=1)
    return jnp.concatenate([row, row], axis=0)


def picked(x, b, odd):
    return jnp.concatenate([x[i : i + b] for i in range(odd * b, 128, 2 * b)], axis=0)


def woven(even, odd, b):
    parts = []
    for i in range(0, 64, b):
        parts += [even[i : i + b], odd[i : i + b]]
    return jnp.concatenate(parts, axis=0)


def log_beta(x):
    return -(jnp.maximum(-x, 0.0) + jnp.log1p(jnp.exp(-jnp.abs(x))))


def prod(left, right):
    if MODE == 0:
        return fold(mm(left, jnp.concatenate([right, right], axis=0)))
    m = left.shape[0]
    r = mm(jnp.concatenate([left[:, :128], left[:, 128:]], axis=0), right)
    return r[:m, :128] + r[:m, 128:] + r[m:, :128]


def unpack(p):
    return p[:, :128].astype(F32) + p[:, 128:].astype(F32)


def running_sum(x):
    r = lax.broadcasted_iota(jnp.int32, (256, 256), 0)
    c = lax.broadcasted_iota(jnp.int32, (256, 256), 1)
    tri = jnp.where(r <= c, 1.0, 0.0).astype(BF16)
    parts = jnp.concatenate([p.astype(F32) for p in split3(x)] + [jnp.zeros((8, 256), F32)], axis=0)
    y = mm(parts.astype(BF16), tri)
    return y[:8] + y[8:16] + y[16:24]


def spans(left, right):
    ones = jnp.ones((24, 256), F32)
    lhs = jnp.concatenate([p.astype(F32) for p in split3(left)] + [ones, jnp.zeros((80, 256), F32)], axis=0)
    cols = lhs.T.astype(BF16)[:, :64]
    rhs = jnp.concatenate([ones] + [p.astype(F32) for p in split3(-right)] + [jnp.zeros((16, 256), F32)], axis=0)
    at = lax.broadcasted_iota(jnp.int32, (64, 256), 0) % 8
    return cols, lambda h: jnp.where(at == h, rhs, 0.0).astype(BF16)


def maps_kernel(
    tb, slot_hbm, k_hbm, v_hbm, g_hbm, b_hbm, pay_ref, keep_ref, x_ref, l21, slot_ref,
    kr, vr, gr, br, kf, vf, kks, kt, rows, l11, l22, p11, p22, cmp_ref, xc, bb, mid, sems,
):
    copies = [
        pltpu.make_async_copy(src, dst, sems.at[i])
        for i, (src, dst) in enumerate([(k_hbm, kr), (g_hbm, gr), (b_hbm, br), (v_hbm, vr), (slot_hbm, slot_ref)])
    ]
    for c in copies:
        c.start()
    ctx = lax.axis_index("ctx")
    row = lax.broadcasted_iota(jnp.int32, (128, 128), 0)
    col = lax.broadcasted_iota(jnp.int32, (128, 128), 1)
    lower = row > col
    eye = row == col
    copies[1].wait()
    copies[2].wait()
    edge = tb[0] * 128 - ctx * 256
    live = lax.broadcasted_iota(jnp.int32, (8, 256), 1) < edge
    gate = gr[...]
    steps = -(jnp.maximum(gate, 0.0) + jnp.log1p(jnp.exp(-jnp.abs(gate))))
    G = running_sum(jnp.where(live, steps, 0.0))
    lb = log_beta(br[...])
    last = G[:, 255:256]
    rows[1] = jnp.where(live, jnp.exp(lb), 0.0)
    rows[3] = jnp.broadcast_to(jnp.exp(last), (8, 256))
    early = G + jnp.where(live, lb, -1e4)
    copies[0].wait()
    kf[...] = kr[...].astype(F32)
    norms = []
    for kh in range(4):
        kx = kf[pl.ds(kh, 256, stride=4), :]
        k = kx.astype(BF16)
        kt[kh] = kx.T
        kk1 = mm_nt(k[:128], k[:128])
        kk2 = mm_nt(k[128:], k)
        kks[kh, :128, :128] = kk1
        kks[kh, 128:] = kk2
        s1 = jnp.sum(jnp.where(eye, kk1, 0.0), axis=0, keepdims=True)
        s2 = jnp.sum(jnp.where(eye, kk2[:, 128:], 0.0), axis=0, keepdims=True)
        norms.append(jnp.concatenate([s1, s2], axis=1))
    ln = -0.5 * jnp.log(jnp.concatenate([norms[h // 2] for h in range(8)], axis=0) + 1e-06)
    a = early + ln
    rows[0] = jnp.exp(a)
    rows[2] = jnp.exp(last - G + ln)
    cols, right = spans(a, G - ln)
    for h in range(8):
        kh = h // 2
        r = right(h)
        d1 = mm(cols[:128], r[:, :128])
        d2 = mm(cols[128:], r)
        t11 = jnp.where(lower, jnp.exp(d1) * kks[kh, :128, :128], 0.0)
        t22 = jnp.where(lower, jnp.exp(d2[:, 128:]) * kks[kh, 128:, 128:], 0.0)
        l11[h] = t11
        l22[h] = t22
        p11[h] = pack_left(t11)
        p22[h] = pack_left(t22)
        l21[h] = pack_left(jnp.exp(d2[:, :128]) * kks[kh, 128:, :128])

    group = lax.broadcasted_iota(jnp.int32, (16, 128), 1) // 16
    for kb in range(16):
        src = l11 if kb < 8 else l22
        r0 = (kb % 8) * 16
        acc = jnp.zeros((16, 128), F32)
        for q in range(8):
            t = src[q, r0 : r0 + 16, :]
            shift = (q * 16 - r0) % 128
            if shift:
                t = pltpu.roll(t, shift, 1)
            acc = jnp.where(group == q, t, acc)
        cmp_ref[kb * 16 : kb * 16 + 16, :] = acc

    copies[3].wait()
    copies[4].wait()
    vf[...] = vr[...].astype(F32)
    lane = lax.broadcasted_iota(jnp.int32, (16, 128), 1)
    base = (lane // 16) * 16
    xs = [jnp.where(lane % 16 == i, 1.0, 0.0).astype(F32) for i in range(16)]
    ls = [cmp_ref[pl.ds(i, 16, stride=16), :] for i in range(16)]
    for j in range(16):
        xc[pl.ds(j, 16, stride=16), :] = xs[j]
        for i in range(j + 1, 16):
            coef = jnp.take_along_axis(ls[i], base + j, axis=1, mode="promise_in_bounds")
            xs[i] = xs[i] - coef * xs[j]

    block = row // 16 == col // 16
    if EXPAND == 0:
        col16, block16 = col[:EG] % 16, [row[i : i + EG] // 16 == col[i : i + EG] // 16 for i in range(0, 128, EG)]
        for part in range(2):
            for i in range(0, 128, EG):
                x = xc[part * 128 + i : part * 128 + i + EG, :]
                ys = [jnp.take_along_axis(x, h * 16 + col16, axis=1, mode="promise_in_bounds") for h in range(8)]
                ys = [pack_left(jnp.where(block16[i // EG], y, 0.0)) for y in ys]
                for h in range(8):
                    x_ref[h, part, i : i + EG] = ys[h]
    else:
        src = lax.broadcasted_iota(jnp.int32, (128, 256), 0)
        dst = lax.broadcasted_iota(jnp.int32, (128, 256), 1)
        both = jnp.concatenate(split(xc[...]), axis=0)
        for p in range(4):
            pick = jnp.where(src == (2 * p + dst // 128) * 16 + dst % 16, 1.0, 0.0).astype(BF16)
            r = mm(both, pick)
            for s in range(2):
                for part in range(2):
                    hi = jnp.where(block, r[part * 128 : part * 128 + 128, s * 128 : s * 128 + 128], 0.0)
                    lo = jnp.where(block, r[256 + part * 128 : 384 + part * 128, s * 128 : s * 128 + 128], 0.0)
                    x_ref[2 * p + s, part, :, :128] = hi.astype(BF16)
                    x_ref[2 * p + s, part, :, 128:] = lo.astype(BF16)
    halfrow = lax.broadcasted_iota(jnp.int32, (64, 256), 0)
    halfcol = lax.broadcasted_iota(jnp.int32, (64, 256), 1) % 128
    zero = jnp.zeros((64, 256), BF16)
    for b in (16, 32, 64):
        under = halfcol // b == (halfrow // b) * 2
        pairs = [(h, part, src) for h in range(8) for part, src in ((0, p11), (1, p22))]
        for h, part, src in pairs:
            l = jnp.where(under, picked(src[h], b, 1), zero)
            mid[h, part] = pack_left(prod(l, x_ref[h, part]))
        for h, part, src in pairs:
            odd = picked(x_ref[h, part], b, 1)
            new = pack_left(unpack(odd) - prod(odd, woven(zero, mid[h, part], b)))
            for i in range(0, 64, b):
                x_ref[h, part, 2 * i + b : 2 * i + 2 * b] = new[i : i + b]

    for h in range(8):
        ktz = kt[h // 2] * rows[2, h : h + 1, :]
        b2 = prod(pack_left(ktz[:, 128:]), x_ref[h, 1])
        bb[h, :, 128:] = b2
        l11[h] = ktz[:, :128]
        p22[h] = pack_left(b2)
    for h in range(8):
        p11[h] = pack_left(l11[h] - prod(p22[h], l21[h]))
    for h in range(8):
        bb[h, :, :128] = prod(p11[h], x_ref[h, 0])
    for h in range(8):
        k = kf[pl.ds((h // 2), 256, stride=4), :].astype(BF16)
        t = mm(jnp.concatenate(split(bb[h] * rows[0, h : h + 1, :]), axis=0), k)
        t = jnp.where(eye, rows[3, h : h + 1, :128], 0.0) - (t[:128] + t[128:])
        l11[h] = t
        keep_ref[h, :64] = t[64:]
    for h in range(8):
        v = vf[pl.ds(h, 256, stride=8), :].astype(BF16)
        u = mm(jnp.concatenate(split(bb[h] * rows[1, h : h + 1, :]), axis=0), v)
        u = u[:128] + u[128:]
        keep_ref[h, 64:] = u[64:]
        pay_ref[h] = jnp.where(ctx == 0, u, jnp.concatenate([l11[h, :64], u[:64]], axis=0))


HEADS_PER_STEP = 4


def vm():
    return pl.BlockSpec(memory_space=pltpu.VMEM)


def sm():
    return pl.BlockSpec(memory_space=pltpu.SMEM)


def hbm():
    return pl.BlockSpec(memory_space=pltpu.HBM)


VL = 24
MODE = 0
EG = 16
EXPAND = 0


def maps(tb, slot_map, k, v, g, b):
    big = lambda *s: pltpu.VMEM(s, F32)
    return pl.pallas_call(
        maps_kernel,
        out_shape=[
            pltpu.VMEM((8, 128, 128), F32),
            pltpu.VMEM((8, 128, 128), F32),
            pltpu.VMEM((8, 2, 128, 256), BF16),
            pltpu.VMEM((8, 128, 256), BF16),
            pltpu.SMEM((32,), jnp.int32),
        ],
        in_specs=[sm()] + [hbm()] * 5,
        out_specs=[vm()] * 4 + [sm()],
        scratch_shapes=[
            pltpu.VMEM((1024, 128), BF16), pltpu.VMEM((2048, 128), BF16), big(8, 256), big(8, 256),
            big(1024, 128), big(2048, 128), big(4, 256, 256), big(4, 128, 256), big(4, 8, 256),
            big(8, 128, 128), big(8, 128, 128),
            pltpu.VMEM((8, 128, 256), BF16), pltpu.VMEM((8, 128, 256), BF16),
            big(256, 128), big(256, 128), big(8, 128, 256), pltpu.VMEM((8, 2, 64, 256), BF16),
            pltpu.SemaphoreType.DMA((5,)),
        ],
        compiler_params=pltpu.CompilerParams(vmem_limit_bytes=VL * 2**20),
        name="maps",
    )(tb, *[pltpu.with_memory_space_constraint(a, pltpu.HBM) for a in (slot_map, k, v, g, b)])


def final_kernel(pay_ref, keep_ref, got_ref, out_ref):
    def work(a_ref, m_ref):
        for h in range(8):
            out_ref[pl.ds(h * 64, 64), :] = mm_small(a_ref[h, :64], m_ref[h]) + a_ref[h, 64:]

    first = lax.axis_index("ctx") == 0

    @pl.when(first)
    def _():
        work(got_ref, pay_ref)

    @pl.when(jnp.logical_not(first))
    def _():
        work(keep_ref, got_ref)


def final(pay, keep, got):
    return pl.pallas_call(
        final_kernel,
        out_shape=pltpu.VMEM((512, 128), F32),
        in_specs=[vm(), vm(), vm()],
        out_specs=vm(),
        compiler_params=pltpu.CompilerParams(vmem_limit_bytes=16 * 2**20),
        name="final",
    )(pay, keep, got)


def reads_kernel(tb, q_ref, k_ref, v_ref, g_ref, b_ref, x_ref, l_ref, m_ref, o_ref, qf, kf, vf, rcol, bcol, ecol, of):
    qf[...] = q_ref[...].astype(F32)
    kf[...] = k_ref[...].astype(F32)
    vf[...] = v_ref[...].astype(F32)
    ctx = lax.axis_index("ctx")
    edge = tb[0] * 128 - ctx * 256
    live = lax.broadcasted_iota(jnp.int32, (8, 256), 1) < edge
    G = decay_rows(g_ref[...], live)
    lb = log_beta(b_ref[...])
    lane = lax.broadcasted_iota(jnp.int32, (256, 128), 1)
    norms = jnp.zeros((256, 128), F32)
    for kh in range(4):
        nk = log_norm(kf[pl.ds(kh, 256, stride=4), :])
        nq = log_norm(qf[pl.ds(kh, 256, stride=4), :])
        for h in (2 * kh, 2 * kh + 1):
            norms = jnp.where(lane == h, nk, norms)
            norms = jnp.where(lane == 8 + h, nq, norms)
    norm_rows = norms.T
    nk, nq = norm_rows[:8], norm_rows[8:16]
    p = G + nq
    a = G + nk + jnp.where(live, lb, -1e4)
    scale = to_columns(jnp.concatenate([jnp.exp(a), jnp.where(live, jnp.exp(lb), 0.0), jnp.exp(p)], axis=0))
    for h in range(8):
        rcol[h] = jnp.broadcast_to(scale[:, h : h + 1], (256, 128))
        bcol[h] = jnp.broadcast_to(scale[:, 8 + h : 9 + h], (256, 128))
        ecol[h] = jnp.broadcast_to(scale[:, 16 + h : 17 + h], (256, 128))
    cols, right = spans(p, G - nk)
    row = lax.broadcasted_iota(jnp.int32, (128, 128), 0)
    col = lax.broadcasted_iota(jnp.int32, (128, 128), 1)
    lower = row >= col
    has = (ctx != 0).astype(F32)
    live1, live2 = edge > 0, edge > 128
    def one(kh, c):
        k = kf[pl.ds(kh, 256, stride=4), :].astype(BF16)
        q = qf[pl.ds(kh, 256, stride=4), :].astype(BF16)
        qk1 = mm_nt(q[:128], k[:128])
        qk2 = mm_nt(q[128:], k)
        kq = jnp.concatenate([k, q], axis=0)
        for j in range(2):
            h = 2 * kh + j
            mrow = jnp.concatenate(split(m_ref[h] * has), axis=1)
            km = fold(mm(kq, mrow))
            d = bcol[h] * vf[pl.ds(h, 256, stride=8), :] - rcol[h] * km[:256]
            d1 = prod(x_ref[h, 0], pack_left(d[:128]))
            d2 = prod(x_ref[h, 1], pack_left(d[128:] - prod(l_ref[h], pack_left(d1))))
            qm = km[256:] * ecol[h]
            r = right(h)
            e1 = mm(cols[:128], r[:, :128])
            e2 = mm(cols[128:], r)
            p11 = jnp.where(lower, jnp.exp(e1) * qk1, 0.0)
            p21 = jnp.exp(e2[:, :128]) * qk2[:, :128]
            p22 = jnp.where(lower, jnp.exp(e2[:, 128:]) * qk2[:, 128:], 0.0)
            o1 = qm[:128] + mm_small(p11, d1)
            ph, pl_ = split(jnp.concatenate([p21, p22], axis=1))
            dh, dl = split(jnp.concatenate([d1, d2], axis=0))
            o2 = qm[128:] + fold(mm(ph, jnp.concatenate([dh, dl], axis=1))) + mm(pl_, dh)
            o1 = jnp.where(live1, o1, 0.0)
            o2 = jnp.where(live2, o2, 0.0)
            of[pl.ds(h, 256, stride=8), :] = jnp.concatenate([o1, o2], axis=0)
        return c

    lax.fori_loop(0, 4, one, 0)
    o_ref[...] = of[...].astype(BF16)


def reads(tb, q, k, v, g, b, x, l, m):
    big = lambda *s: pltpu.VMEM(s, F32)
    return pl.pallas_call(
        reads_kernel,
        out_shape=jax.ShapeDtypeStruct((2048, 128), BF16),
        in_specs=[sm()] + [vm()] * 8,
        out_specs=vm(),
        scratch_shapes=[
            big(1024, 128), big(1024, 128), big(2048, 128),
            big(8, 256, 128), big(8, 256, 128), big(8, 256, 128), big(2048, 128),
        ],
        compiler_params=pltpu.CompilerParams(vmem_limit_bytes=24 * 2**20),
        cost_estimate=pl.CostEstimate(flops=8 * 4 * 2 * 256**3, bytes_accessed=4 * 2**20, transcendentals=0),
        name="reads",
    )(tb, q, k, v, g, b, x, l, m)


def reorder_kernel(slot_ref, in_ref, out_ref):
    for s in range(32):
        out_ref[slot_ref[s]] = in_ref[s]


def reorder(slot_map, x):
    return pl.pallas_call(
        reorder_kernel,
        out_shape=pltpu.VMEM(x.shape, x.dtype),
        in_specs=[sm(), vm()],
        out_specs=vm(),
        name="reorder",
    )(
        pltpu.with_memory_space_constraint(slot_map, pltpu.SMEM),
        pltpu.with_memory_space_constraint(x, pltpu.VMEM),
    )


def place_kernel(in_ref, out_hbm, sem):
    copy = pltpu.make_async_copy(in_ref, out_hbm, sem)
    copy.start()
    copy.wait()


def place(x):
    return pl.pallas_call(
        place_kernel,
        out_shape=jax.ShapeDtypeStruct(x.shape, x.dtype),
        in_specs=[vm()],
        out_specs=hbm(),
        scratch_shapes=[pltpu.SemaphoreType.DMA],
        name="place",
    )(pltpu.with_memory_space_constraint(x, pltpu.VMEM))


def local(queries, keys, values, gate_logit, beta_logit, token_blocks, slot_map):
    q = queries.reshape(1024, 128)
    k = keys.reshape(1024, 128)
    v = values.reshape(2048, 128)
    g = gate_logit.reshape(8, 256)
    b = beta_logit.reshape(8, 256)
    pay, keep, x, l, slots = maps(token_blocks, slot_map, k, v, g, b)
    got = lax.ppermute(pay, "ctx", [(0, 1), (1, 0)])
    rows = final(pay, keep, got)
    spread = lax.all_to_all(rows.reshape(32, 16, 128), "sess", 0, 0, tiled=True)
    out = reads(token_blocks, q, k, v, g, b, x, l, got)
    back = lax.all_to_all(reorder(slots, spread), "sess", 0, 0, tiled=True)
    back = place(back.reshape(1, 8, 64, 128))
    return out.reshape(1, 256, 8, 128), back


def solution(mesh):
    from jax.sharding import PartitionSpec as P
    placed = (
        P("sess", "ctx", "head", None), P("sess", "ctx", "head", None), P("sess", "ctx", "head", None),
        P("sess", "head", "ctx"), P("sess", "head", "ctx"), P("sess"), P(),
    )
    return jax.shard_map(
        local, mesh=mesh, in_specs=placed,
        out_specs=(P("sess", "ctx", "head", None), P("sess", "head", "ctx", None)),
        check_vma=False,
    )
```

```python
import functools
import jax
import jax.numpy as jnp
from jax import lax
from jax.experimental import pallas as pl
from jax.experimental.pallas import tpu as pltpu

F32 = jnp.float32
BF16 = jnp.bfloat16


def split(x):
    hi = x.astype(BF16)
    return hi, (x - hi.astype(F32)).astype(BF16)


def mm(a, b):
    return jnp.dot(a, b, preferred_element_type=F32)


def mm_nt(a, b):
    return lax.dot_general(a, b, (((1,), (1,)), ((), ())), preferred_element_type=F32)


def pack_left(a):
    hi, lo = split(a)
    return jnp.concatenate([hi, lo], axis=1)


def pack_right(b):
    hi, lo = split(b)
    row = jnp.concatenate([hi, lo], axis=1)
    return jnp.concatenate([row, row], axis=0)


def fold(r):
    return r[:, :128] + r[:, 128:]


def mm_small(a, b):
    return fold(mm(pack_left(a), pack_right(b)))


def decay_rows(gate, live):
    x = jnp.where(live, -(jnp.maximum(gate, 0.0) + jnp.log1p(jnp.exp(-jnp.abs(gate)))), 0.0)
    lane = lax.broadcasted_iota(jnp.int32, x.shape, 1)
    step = 1
    while step < 256:
        x = x + jnp.where(lane >= step, pltpu.roll(x, step, 1), 0.0)
        step *= 2
    return x


def to_columns(rows):
    pad = jnp.zeros((128 - rows.shape[0], 256), F32)
    return jnp.concatenate([rows, pad], axis=0).T


def live_lanes(info_ref):
    edge = info_ref[1] * 128 - info_ref[0] * 256
    return lax.broadcasted_iota(jnp.int32, (8, 256), 1) < edge


def log_norm(x):
    return -0.5 * jnp.log(jnp.sum(x * x, axis=1, keepdims=True) + 1e-06)


def split3(x):
    hi = x.astype(BF16)
    r = x - hi.astype(F32)
    mid = r.astype(BF16)
    lo = (r - mid.astype(F32)).astype(BF16)
    return hi, mid, lo


def picked(x, b, odd):
    return jnp.concatenate([x[i : i + b] for i in range(odd * b, 128, 2 * b)], axis=0)


def rows_of(ref, at, b, odd):
    return jnp.concatenate([ref[at + (slice(i, i + b),)] for i in range(odd * b, 128, 2 * b)], axis=0)


def woven(even, odd, b):
    parts = []
    for i in range(0, 64, b):
        parts += [even[i : i + b], odd[i : i + b]]
    return jnp.concatenate(parts, axis=0)


def log_beta(x):
    return -(jnp.maximum(-x, 0.0) + jnp.log1p(jnp.exp(-jnp.abs(x))))


def prod(left, right):
    return fold(mm(left, jnp.concatenate([right, right], axis=0)))


def unpack(p):
    return p[:, :128].astype(F32) + p[:, 128:].astype(F32)


def running_sum(x):
    r = lax.broadcasted_iota(jnp.int32, (256, 256), 0)
    c = lax.broadcasted_iota(jnp.int32, (256, 256), 1)
    tri = jnp.where(r <= c, 1.0, 0.0).astype(BF16)
    parts = jnp.concatenate([p.astype(F32) for p in split3(x)] + [jnp.zeros((8, 256), F32)], axis=0)
    y = mm(parts.astype(BF16), tri)
    return y[:8] + y[8:16] + y[16:24]


def spans(left, right):
    ones = jnp.ones((24, 256), F32)
    lhs = jnp.concatenate([p.astype(F32) for p in split3(left)] + [ones, jnp.zeros((80, 256), F32)], axis=0)
    cols = lhs.T.astype(BF16)[:, :64]
    rhs = jnp.concatenate([ones] + [p.astype(F32) for p in split3(-right)] + [jnp.zeros((16, 256), F32)], axis=0)
    at = lax.broadcasted_iota(jnp.int32, (64, 256), 0) % 8
    return cols, lambda h: jnp.where(at == h, rhs, 0.0).astype(BF16)


def maps_kernel(
    tb, slot_hbm, k_hbm, v_hbm, g_hbm, b_hbm, pay_ref, keep_ref, x_ref, l21, slot_ref,
    kr, vr, gr, br, kf, vf, kks, kt, rows, l11, l22, p11, p22, cmp_ref, xc, sems,
):
    copies = [
        pltpu.make_async_copy(src, dst, sems.at[i])
        for i, (src, dst) in enumerate([(k_hbm, kr), (g_hbm, gr), (b_hbm, br), (v_hbm, vr), (slot_hbm, slot_ref)])
    ]
    for i in (1, 2, 0, 4, 3):
        copies[i].start()
    ctx = lax.axis_index("ctx")
    row = lax.broadcasted_iota(jnp.int32, (128, 128), 0)
    col = lax.broadcasted_iota(jnp.int32, (128, 128), 1)
    lower = row > col
    eye = row == col
    copies[1].wait()
    copies[2].wait()
    edge = tb[0] * 128 - ctx * 256
    live = lax.broadcasted_iota(jnp.int32, (8, 256), 1) < edge
    gate = gr[...]
    steps = -(jnp.maximum(gate, 0.0) + jnp.log1p(jnp.exp(-jnp.abs(gate))))
    G = running_sum(jnp.where(live, steps, 0.0))
    lb = log_beta(br[...])
    last = G[:, 255:256]
    rows[1] = jnp.where(live, jnp.exp(lb), 0.0)
    rows[3] = jnp.broadcast_to(jnp.exp(last), (8, 256))
    early = G + jnp.where(live, lb, -1e4)
    copies[0].wait()
    kf[...] = kr[...].astype(F32)
    norms = []
    for kh in range(4):
        kx = kf[pl.ds(kh, 256, stride=4), :]
        k = kx.astype(BF16)
        kt[kh] = kx.T
        kk1 = mm_nt(k[:128], k[:128])
        kk2 = mm_nt(k[128:], k)
        kks[kh, :128, :128] = kk1
        kks[kh, 128:] = kk2
        s1 = jnp.sum(jnp.where(eye, kk1, 0.0), axis=0, keepdims=True)
        s2 = jnp.sum(jnp.where(eye, kk2[:, 128:], 0.0), axis=0, keepdims=True)
        norms.append(jnp.concatenate([s1, s2], axis=1))
    ln = -0.5 * jnp.log(jnp.concatenate([norms[h // 2] for h in range(8)], axis=0) + 1e-06)
    a = early + ln
    rows[0] = jnp.exp(a)
    rows[2] = jnp.exp(last - G + ln)
    cols, right = spans(a, G - ln)
    for h in range(8):
        kh = h // 2
        r = right(h)
        d1 = mm(cols[:128], r[:, :128])
        d2 = mm(cols[128:], r)
        t11 = jnp.where(lower, jnp.exp(d1) * kks[kh, :128, :128], 0.0)
        t22 = jnp.where(lower, jnp.exp(d2[:, 128:]) * kks[kh, 128:, 128:], 0.0)
        l11[h] = t11
        l22[h] = t22
        p11[h] = pack_left(t11)
        p22[h] = pack_left(t22)
        l21[h] = pack_left(jnp.exp(d2[:, :128]) * kks[kh, 128:, :128])

    group = lax.broadcasted_iota(jnp.int32, (16, 128), 1) // 16
    for kb in range(16):
        src = l11 if kb < 8 else l22
        r0 = (kb % 8) * 16
        acc = jnp.zeros((16, 128), F32)
        for q in range(8):
            t = src[q, r0 : r0 + 16, :]
            shift = (q * 16 - r0) % 128
            if shift:
                t = pltpu.roll(t, shift, 1)
            acc = jnp.where(group == q, t, acc)
        cmp_ref[kb * 16 : kb * 16 + 16, :] = acc

    copies[3].wait()
    copies[4].wait()
    lane = lax.broadcasted_iota(jnp.int32, (16, 128), 1)
    base = (lane // 16) * 16
    xs = [jnp.where(lane % 16 == i, 1.0, 0.0).astype(F32) for i in range(16)]
    ls = [cmp_ref[pl.ds(i, 16, stride=16), :] for i in range(16)]
    for j in range(16):
        xc[pl.ds(j, 16, stride=16), :] = xs[j]
        vf[j * 128 : j * 128 + 128] = vr[j * 128 : j * 128 + 128].astype(F32)
        for i in range(j + 1, 16):
            coef = jnp.take_along_axis(ls[i], base + j, axis=1, mode="promise_in_bounds")
            xs[i] = xs[i] - coef * xs[j]

    col16 = col[:16] % 16
    block16 = [row[i : i + 16] // 16 == col[i : i + 16] // 16 for i in range(0, 128, 16)]
    halfrow = lax.broadcasted_iota(jnp.int32, (64, 256), 0)
    halfcol = lax.broadcasted_iota(jnp.int32, (64, 256), 1) % 128
    zero = jnp.zeros((64, 256), BF16)
    under = {
        b: jnp.where(halfcol // b == (halfrow // b) * 2, 1.0, 0.0).astype(BF16) for b in (16, 32, 64)
    }

    X, MID, TMP, BB = {}, {}, {}, {}

    def expand(h):
        for part in range(2):
            tiles = []
            for i in range(0, 128, 16):
                x = xc[part * 128 + i : part * 128 + i + 16, :]
                x = jnp.take_along_axis(x, h * 16 + col16, axis=1, mode="promise_in_bounds")
                tiles.append(pack_left(jnp.where(block16[i // 16], x, 0.0)))
            X[h, part] = jnp.concatenate(tiles, axis=0)

    def half_one(b):
        def step(h):
            for part, src in ((0, p11), (1, p22)):
                l = rows_of(src, (h,), b, 1) * under[b]
                MID[h, part] = pack_left(prod(l, X[h, part]))

        return step

    def half_two(b):
        def step(h):
            for part in range(2):
                x = X[h, part]
                odd = picked(x, b, 1)
                new = pack_left(unpack(odd) - prod(odd, woven(zero, MID[h, part], b)))
                X[h, part] = woven(picked(x, b, 0), new, b)
                if b == 64:
                    x_ref[h, part] = X[h, part]

        return step

    def right_half(h):
        ktz = kt[h // 2] * rows[2, h : h + 1, :]
        b2 = prod(pack_left(ktz[:, 128:]), X[h, 1])
        BB[h, 1] = b2
        TMP[h, 0] = ktz[:, :128]
        TMP[h, 1] = pack_left(b2)

    def left_rest(h):
        TMP[h, 2] = pack_left(TMP[h, 0] - prod(TMP[h, 1], l21[h]))

    def left_half(h):
        BB[h, 0] = prod(TMP[h, 2], X[h, 0])

    def to_map(h):
        k = kf[pl.ds((h // 2), 256, stride=4), :].astype(BF16)
        bb = jnp.concatenate([BB[h, 0], BB[h, 1]], axis=1)
        t = mm(jnp.concatenate(split(bb * rows[0, h : h + 1, :]), axis=0), k)
        t = jnp.where(eye, rows[3, h : h + 1, :128], 0.0) - (t[:128] + t[128:])
        TMP[h, 3] = t[:64]
        keep_ref[h, :64] = t[64:]

    def to_state(h):
        v = vf[pl.ds(h, 256, stride=8), :].astype(BF16)
        bb = jnp.concatenate([BB[h, 0], BB[h, 1]], axis=1)
        u = mm(jnp.concatenate(split(bb * rows[1, h : h + 1, :]), axis=0), v)
        u = u[:128] + u[128:]
        keep_ref[h, 64:] = u[64:]
        pay_ref[h] = jnp.where(ctx == 0, u, jnp.concatenate([TMP[h, 3], u[:64]], axis=0))

    steps = [expand]
    for b in (16, 32, 64):
        steps += [half_one(b), half_two(b)]
    steps += [right_half, left_rest, left_half, to_map, to_state]
    for step in steps:
        for h in range(8):
            step(h)


def vm():
    return pl.BlockSpec(memory_space=pltpu.VMEM)


def sm():
    return pl.BlockSpec(memory_space=pltpu.SMEM)


def hbm():
    return pl.BlockSpec(memory_space=pltpu.HBM)


def maps(tb, slot_map, k, v, g, b):
    big = lambda *s: pltpu.VMEM(s, F32)
    return pl.pallas_call(
        maps_kernel,
        out_shape=[
            pltpu.VMEM((8, 128, 128), F32),
            pltpu.VMEM((8, 128, 128), F32),
            pltpu.VMEM((8, 2, 128, 256), BF16),
            pltpu.VMEM((8, 128, 256), BF16),
            pltpu.SMEM((32,), jnp.int32),
        ],
        in_specs=[sm()] + [hbm()] * 5,
        out_specs=[vm()] * 4 + [sm()],
        scratch_shapes=[
            pltpu.VMEM((1024, 128), BF16), pltpu.VMEM((2048, 128), BF16), big(8, 256), big(8, 256),
            big(1024, 128), big(2048, 128), big(4, 256, 256), big(4, 128, 256), big(4, 8, 256),
            big(8, 128, 128), big(8, 128, 128),
            pltpu.VMEM((8, 128, 256), BF16), pltpu.VMEM((8, 128, 256), BF16),
            big(256, 128), big(256, 128),
            pltpu.SemaphoreType.DMA((5,)),
        ],
        compiler_params=pltpu.CompilerParams(vmem_limit_bytes=24 * 2**20),
        name="maps",
    )(tb, *[pltpu.with_memory_space_constraint(a, pltpu.HBM) for a in (slot_map, k, v, g, b)])


def final_kernel(pay_ref, keep_ref, got_ref, out_ref):
    def work(a_ref, m_ref):
        for h in range(8):
            out_ref[pl.ds(h * 64, 64), :] = mm_small(a_ref[h, :64], m_ref[h]) + a_ref[h, 64:]

    first = lax.axis_index("ctx") == 0

    @pl.when(first)
    def _():
        work(got_ref, pay_ref)

    @pl.when(jnp.logical_not(first))
    def _():
        work(keep_ref, got_ref)


def final(pay, keep, got):
    return pl.pallas_call(
        final_kernel,
        out_shape=pltpu.VMEM((512, 128), F32),
        in_specs=[vm(), vm(), vm()],
        out_specs=vm(),
        compiler_params=pltpu.CompilerParams(vmem_limit_bytes=16 * 2**20),
        name="final",
    )(pay, keep, got)


def reads_kernel(tb, q_ref, k_ref, v_ref, g_ref, b_ref, x_ref, l_ref, m_ref, o_ref, qf, kf, vf, rcol, bcol, ecol, of):
    qf[...] = q_ref[...].astype(F32)
    kf[...] = k_ref[...].astype(F32)
    vf[...] = v_ref[...].astype(F32)
    ctx = lax.axis_index("ctx")
    edge = tb[0] * 128 - ctx * 256
    live = lax.broadcasted_iota(jnp.int32, (8, 256), 1) < edge
    G = decay_rows(g_ref[...], live)
    lb = log_beta(b_ref[...])
    lane = lax.broadcasted_iota(jnp.int32, (256, 128), 1)
    norms = jnp.zeros((256, 128), F32)
    for kh in range(4):
        nk = log_norm(kf[pl.ds(kh, 256, stride=4), :])
        nq = log_norm(qf[pl.ds(kh, 256, stride=4), :])
        for h in (2 * kh, 2 * kh + 1):
            norms = jnp.where(lane == h, nk, norms)
            norms = jnp.where(lane == 8 + h, nq, norms)
    norm_rows = norms.T
    nk, nq = norm_rows[:8], norm_rows[8:16]
    p = G + nq
    a = G + nk + jnp.where(live, lb, -1e4)
    scale = to_columns(jnp.concatenate([jnp.exp(a), jnp.where(live, jnp.exp(lb), 0.0), jnp.exp(p)], axis=0))
    for h in range(8):
        rcol[h] = jnp.broadcast_to(scale[:, h : h + 1], (256, 128))
        bcol[h] = jnp.broadcast_to(scale[:, 8 + h : 9 + h], (256, 128))
        ecol[h] = jnp.broadcast_to(scale[:, 16 + h : 17 + h], (256, 128))
    cols, right = spans(p, G - nk)
    row = lax.broadcasted_iota(jnp.int32, (128, 128), 0)
    col = lax.broadcasted_iota(jnp.int32, (128, 128), 1)
    lower = row >= col
    has = (ctx != 0).astype(F32)
    live1, live2 = edge > 0, edge > 128
    for kh in range(4):
        k = kf[pl.ds(kh, 256, stride=4), :].astype(BF16)
        q = qf[pl.ds(kh, 256, stride=4), :].astype(BF16)
        qk1 = mm_nt(q[:128], k[:128])
        qk2 = mm_nt(q[128:], k)
        kq = jnp.concatenate([k, q], axis=0)
        for h in (2 * kh, 2 * kh + 1):
            mrow = jnp.concatenate(split(m_ref[h] * has), axis=1)
            km = fold(mm(kq, mrow))
            d = bcol[h] * vf[pl.ds(h, 256, stride=8), :] - rcol[h] * km[:256]
            d1 = prod(x_ref[h, 0], pack_left(d[:128]))
            d2 = prod(x_ref[h, 1], pack_left(d[128:] - prod(l_ref[h], pack_left(d1))))
            qm = km[256:] * ecol[h]
            r = right(h)
            e1 = mm(cols[:128], r[:, :128])
            e2 = mm(cols[128:], r)
            p11 = jnp.where(lower, jnp.exp(e1) * qk1, 0.0)
            p21 = jnp.exp(e2[:, :128]) * qk2[:, :128]
            p22 = jnp.where(lower, jnp.exp(e2[:, 128:]) * qk2[:, 128:], 0.0)
            o1 = qm[:128] + mm_small(p11, d1)
            ph, pl_ = split(jnp.concatenate([p21, p22], axis=1))
            dh, dl = split(jnp.concatenate([d1, d2], axis=0))
            o2 = qm[128:] + fold(mm(ph, jnp.concatenate([dh, dl], axis=1))) + mm(pl_, dh)
            o1 = jnp.where(live1, o1, 0.0)
            o2 = jnp.where(live2, o2, 0.0)
            of[pl.ds(h, 256, stride=8), :] = jnp.concatenate([o1, o2], axis=0)
    o_ref[...] = of[...].astype(BF16)


def reads(tb, q, k, v, g, b, x, l, m):
    big = lambda *s: pltpu.VMEM(s, F32)
    return pl.pallas_call(
        reads_kernel,
        out_shape=jax.ShapeDtypeStruct((2048, 128), BF16),
        in_specs=[sm()] + [vm()] * 8,
        out_specs=vm(),
        scratch_shapes=[
            big(1024, 128), big(1024, 128), big(2048, 128),
            big(8, 256, 128), big(8, 256, 128), big(8, 256, 128), big(2048, 128),
        ],
        compiler_params=pltpu.CompilerParams(vmem_limit_bytes=24 * 2**20),
        cost_estimate=pl.CostEstimate(flops=8 * 4 * 2 * 256**3, bytes_accessed=4 * 2**20, transcendentals=0),
        name="reads",
    )(tb, q, k, v, g, b, x, l, m)


def reorder_kernel(slot_ref, in_ref, out_ref):
    for s in range(32):
        out_ref[slot_ref[s]] = in_ref[s]


def reorder(slot_map, x):
    return pl.pallas_call(
        reorder_kernel,
        out_shape=pltpu.VMEM(x.shape, x.dtype),
        in_specs=[sm(), vm()],
        out_specs=vm(),
        name="reorder",
    )(
        pltpu.with_memory_space_constraint(slot_map, pltpu.SMEM),
        pltpu.with_memory_space_constraint(x, pltpu.VMEM),
    )


def place_kernel(in_ref, out_hbm, sem):
    copy = pltpu.make_async_copy(in_ref, out_hbm, sem)
    copy.start()
    copy.wait()


def place(x):
    return pl.pallas_call(
        place_kernel,
        out_shape=jax.ShapeDtypeStruct(x.shape, x.dtype),
        in_specs=[vm()],
        out_specs=hbm(),
        scratch_shapes=[pltpu.SemaphoreType.DMA],
        name="place",
    )(pltpu.with_memory_space_constraint(x, pltpu.VMEM))


def local(queries, keys, values, gate_logit, beta_logit, token_blocks, slot_map):
    q = queries.reshape(1024, 128)
    k = keys.reshape(1024, 128)
    v = values.reshape(2048, 128)
    g = gate_logit.reshape(8, 256)
    b = beta_logit.reshape(8, 256)
    pay, keep, x, l, slots = maps(token_blocks, slot_map, k, v, g, b)
    got = lax.ppermute(pay, "ctx", [(0, 1), (1, 0)])
    rows = final(pay, keep, got)
    spread = lax.all_to_all(rows.reshape(32, 16, 128), "sess", 0, 0, tiled=True)
    out = reads(token_blocks, q, k, v, g, b, x, l, got)
    back = lax.all_to_all(reorder(slots, spread), "sess", 0, 0, tiled=True)
    back = place(back.reshape(1, 8, 64, 128))
    return out.reshape(1, 256, 8, 128), back


def solution(mesh):
    from jax.sharding import PartitionSpec as P
    placed = (
        P("sess", "ctx", "head", None), P("sess", "ctx", "head", None), P("sess", "ctx", "head", None),
        P("sess", "head", "ctx"), P("sess", "head", "ctx"), P("sess"), P(),
    )
    return jax.shard_map(
        local, mesh=mesh, in_specs=placed,
        out_specs=(P("sess", "ctx", "head", None), P("sess", "head", "ctx", None)),
        check_vma=False,
    )
```

```python
import functools
import jax
import jax.numpy as jnp
from jax import lax
from jax.experimental import pallas as pl
from jax.experimental.pallas import tpu as pltpu

F32 = jnp.float32
BF16 = jnp.bfloat16


def split(x):
    hi = x.astype(BF16)
    return hi, (x - hi.astype(F32)).astype(BF16)


def mm(a, b):
    return jnp.dot(a, b, preferred_element_type=F32)


def mm_nt(a, b):
    return lax.dot_general(a, b, (((1,), (1,)), ((), ())), preferred_element_type=F32)


def pack_left(a):
    hi, lo = split(a)
    return jnp.concatenate([hi, lo], axis=1)


def pack_right(b):
    hi, lo = split(b)
    row = jnp.concatenate([hi, lo], axis=1)
    return jnp.concatenate([row, row], axis=0)


def fold(r):
    return r[:, :128] + r[:, 128:]


def mm_small(a, b):
    return fold(mm(pack_left(a), pack_right(b)))


def decay_rows(gate, live):
    x = jnp.where(live, -(jnp.maximum(gate, 0.0) + jnp.log1p(jnp.exp(-jnp.abs(gate)))), 0.0)
    lane = lax.broadcasted_iota(jnp.int32, x.shape, 1)
    step = 1
    while step < 256:
        x = x + jnp.where(lane >= step, pltpu.roll(x, step, 1), 0.0)
        step *= 2
    return x


def to_columns(rows):
    pad = jnp.zeros((128 - rows.shape[0], 256), F32)
    return jnp.concatenate([rows, pad], axis=0).T


def live_lanes(info_ref):
    edge = info_ref[1] * 128 - info_ref[0] * 256
    return lax.broadcasted_iota(jnp.int32, (8, 256), 1) < edge


def log_norm(x):
    return -0.5 * jnp.log(jnp.sum(x * x, axis=1, keepdims=True) + 1e-06)


def split3(x):
    hi = x.astype(BF16)
    r = x - hi.astype(F32)
    mid = r.astype(BF16)
    lo = (r - mid.astype(F32)).astype(BF16)
    return hi, mid, lo


def picked(x, b, odd):
    return jnp.concatenate([x[i : i + b] for i in range(odd * b, 128, 2 * b)], axis=0)


def rows_of(ref, at, b, odd):
    return jnp.concatenate([ref[at + (slice(i, i + b),)] for i in range(odd * b, 128, 2 * b)], axis=0)


def woven(even, odd, b):
    parts = []
    for i in range(0, 64, b):
        parts += [even[i : i + b], odd[i : i + b]]
    return jnp.concatenate(parts, axis=0)


def log_beta(x):
    return -(jnp.maximum(-x, 0.0) + jnp.log1p(jnp.exp(-jnp.abs(x))))


def prod(left, right):
    return fold(mm(left, jnp.concatenate([right, right], axis=0)))


def unpack(p):
    return p[:, :128].astype(F32) + p[:, 128:].astype(F32)


def running_sum(x):
    r = lax.broadcasted_iota(jnp.int32, (256, 256), 0)
    c = lax.broadcasted_iota(jnp.int32, (256, 256), 1)
    tri = jnp.where(r <= c, 1.0, 0.0).astype(BF16)
    parts = jnp.concatenate([p.astype(F32) for p in split3(x)] + [jnp.zeros((8, 256), F32)], axis=0)
    y = mm(parts.astype(BF16), tri)
    return y[:8] + y[8:16] + y[16:24]


def spans(left, right):
    ones = jnp.ones((24, 256), F32)
    lhs = jnp.concatenate([p.astype(F32) for p in split3(left)] + [ones, jnp.zeros((80, 256), F32)], axis=0)
    cols = lhs.T.astype(BF16)[:, :64]
    rhs = jnp.concatenate([ones] + [p.astype(F32) for p in split3(-right)] + [jnp.zeros((16, 256), F32)], axis=0)
    at = lax.broadcasted_iota(jnp.int32, (64, 256), 0) % 8
    return cols, lambda h: jnp.where(at == h, rhs, 0.0).astype(BF16)


def maps_kernel(
    tb, slot_hbm, k_hbm, v_hbm, g_hbm, b_hbm, pay_ref, keep_ref, x_ref, l21, slot_ref,
    kr, vr, gr, br, kf, vf, kks, kt, rows, l11, l22, p11, p22, cmp_ref, xc, sems,
):
    copies = [
        pltpu.make_async_copy(src, dst, sems.at[i])
        for i, (src, dst) in enumerate([(k_hbm, kr), (g_hbm, gr), (b_hbm, br), (v_hbm, vr), (slot_hbm, slot_ref)])
    ]
    for i in (1, 2, 0, 4, 3):
        copies[i].start()
    ctx = lax.axis_index("ctx")
    row = lax.broadcasted_iota(jnp.int32, (128, 128), 0)
    col = lax.broadcasted_iota(jnp.int32, (128, 128), 1)
    lower = row > col
    eye = row == col
    copies[1].wait()
    copies[2].wait()
    edge = tb[0] * 128 - ctx * 256
    live = lax.broadcasted_iota(jnp.int32, (8, 256), 1) < edge
    gate = gr[...]
    steps = -(jnp.maximum(gate, 0.0) + jnp.log1p(jnp.exp(-jnp.abs(gate))))
    G = running_sum(jnp.where(live, steps, 0.0))
    lb = log_beta(br[...])
    last = G[:, 255:256]
    rows[1] = jnp.where(live, jnp.exp(lb), 0.0)
    rows[3] = jnp.broadcast_to(jnp.exp(last), (8, 256))
    early = G + jnp.where(live, lb, -1e4)
    copies[0].wait()
    kf[...] = kr[...].astype(F32)
    norms = []
    for kh in range(4):
        kx = kf[pl.ds(kh, 256, stride=4), :]
        k = kx.astype(BF16)
        kt[kh] = kx.T
        kk1 = mm_nt(k[:128], k[:128])
        kk2 = mm_nt(k[128:], k)
        kks[kh, :128, :128] = kk1
        kks[kh, 128:] = kk2
        s1 = jnp.sum(jnp.where(eye, kk1, 0.0), axis=0, keepdims=True)
        s2 = jnp.sum(jnp.where(eye, kk2[:, 128:], 0.0), axis=0, keepdims=True)
        norms.append(jnp.concatenate([s1, s2], axis=1))
    ln = -0.5 * jnp.log(jnp.concatenate([norms[h // 2] for h in range(8)], axis=0) + 1e-06)
    a = early + ln
    rows[0] = jnp.exp(a)
    rows[2] = jnp.exp(last - G + ln)
    cols, right = spans(a, G - ln)
    for h in range(8):
        kh = h // 2
        r = right(h)
        d1 = mm(cols[:128], r[:, :128])
        d2 = mm(cols[128:], r)
        t11 = jnp.where(lower, jnp.exp(d1) * kks[kh, :128, :128], 0.0)
        t22 = jnp.where(lower, jnp.exp(d2[:, 128:]) * kks[kh, 128:, 128:], 0.0)
        l11[h] = t11
        l22[h] = t22
        p11[h] = pack_left(t11)
        p22[h] = pack_left(t22)
        l21[h] = pack_left(jnp.exp(d2[:, :128]) * kks[kh, 128:, :128])

    group = lax.broadcasted_iota(jnp.int32, (16, 128), 1) // 16
    for kb in range(16):
        src = l11 if kb < 8 else l22
        r0 = (kb % 8) * 16
        acc = jnp.zeros((16, 128), F32)
        for q in range(8):
            t = src[q, r0 : r0 + 16, :]
            shift = (q * 16 - r0) % 128
            if shift:
                t = pltpu.roll(t, shift, 1)
            acc = jnp.where(group == q, t, acc)
        cmp_ref[kb * 16 : kb * 16 + 16, :] = acc

    copies[3].wait()
    copies[4].wait()
    lane = lax.broadcasted_iota(jnp.int32, (16, 128), 1)
    base = (lane // 16) * 16
    xs = [jnp.where(lane % 16 == i, 1.0, 0.0).astype(F32) for i in range(16)]
    ls = [cmp_ref[pl.ds(i, 16, stride=16), :] for i in range(16)]
    for j in range(16):
        xc[pl.ds(j, 16, stride=16), :] = xs[j]
        vf[j * 128 : j * 128 + 128] = vr[j * 128 : j * 128 + 128].astype(F32)
        for i in range(j + 1, 16):
            coef = jnp.take_along_axis(ls[i], base + j, axis=1, mode="promise_in_bounds")
            xs[i] = xs[i] - coef * xs[j]

    col16 = col[:16] % 16
    block16 = [row[i : i + 16] // 16 == col[i : i + 16] // 16 for i in range(0, 128, 16)]
    halfrow = lax.broadcasted_iota(jnp.int32, (64, 256), 0)
    halfcol = lax.broadcasted_iota(jnp.int32, (64, 256), 1) % 128
    zero = jnp.zeros((64, 256), BF16)
    under = {
        b: jnp.where(halfcol // b == (halfrow // b) * 2, 1.0, 0.0).astype(BF16) for b in (16, 32, 64)
    }

    X, MID, TMP, BB = {}, {}, {}, {}

    def expand(h):
        for part in range(2):
            tiles = []
            for i in range(0, 128, 16):
                x = xc[part * 128 + i : part * 128 + i + 16, :]
                x = jnp.take_along_axis(x, h * 16 + col16, axis=1, mode="promise_in_bounds")
                tiles.append(pack_left(jnp.where(block16[i // 16], x, 0.0)))
            X[h, part] = jnp.concatenate(tiles, axis=0)

    def half_one(b):
        def step(h):
            for part, src in ((0, p11), (1, p22)):
                l = rows_of(src, (h,), b, 1) * under[b]
                MID[h, part] = pack_left(prod(l, X[h, part]))

        return step

    def half_two(b):
        def step(h):
            for part in range(2):
                x = X[h, part]
                odd = picked(x, b, 1)
                new = pack_left(unpack(odd) - prod(odd, woven(zero, MID[h, part], b)))
                X[h, part] = woven(picked(x, b, 0), new, b)
                if b == 64:
                    x_ref[h, part] = X[h, part]

        return step

    def right_half(h):
        ktz = kt[h // 2] * rows[2, h : h + 1, :]
        b2 = prod(pack_left(ktz[:, 128:]), X[h, 1])
        BB[h, 1] = b2
        TMP[h, 0] = ktz[:, :128]
        TMP[h, 1] = pack_left(b2)

    def left_rest(h):
        TMP[h, 2] = pack_left(TMP[h, 0] - prod(TMP[h, 1], l21[h]))

    def left_half(h):
        BB[h, 0] = prod(TMP[h, 2], X[h, 0])

    def to_map(h):
        k = kf[pl.ds((h // 2), 256, stride=4), :].astype(BF16)
        bb = jnp.concatenate([BB[h, 0], BB[h, 1]], axis=1)
        t = mm(jnp.concatenate(split(bb * rows[0, h : h + 1, :]), axis=0), k)
        t = jnp.where(eye, rows[3, h : h + 1, :128], 0.0) - (t[:128] + t[128:])
        TMP[h, 3] = t[:64]
        keep_ref[h, :64] = t[64:]

    def to_state(h):
        v = vf[pl.ds(h, 256, stride=8), :].astype(BF16)
        bb = jnp.concatenate([BB[h, 0], BB[h, 1]], axis=1)
        u = mm(jnp.concatenate(split(bb * rows[1, h : h + 1, :]), axis=0), v)
        u = u[:128] + u[128:]
        keep_ref[h, 64:] = u[64:]
        pay_ref[h] = jnp.where(ctx == 0, u, jnp.concatenate([TMP[h, 3], u[:64]], axis=0))

    steps = [expand]
    for b in (16, 32, 64):
        steps += [half_one(b), half_two(b)]
    steps += [right_half, left_rest, left_half, to_map, to_state]
    for step in steps:
        for h in range(8):
            step(h)


def vm():
    return pl.BlockSpec(memory_space=pltpu.VMEM)


def sm():
    return pl.BlockSpec(memory_space=pltpu.SMEM)


def hbm():
    return pl.BlockSpec(memory_space=pltpu.HBM)


def maps(tb, slot_map, k, v, g, b):
    big = lambda *s: pltpu.VMEM(s, F32)
    return pl.pallas_call(
        maps_kernel,
        out_shape=[
            pltpu.VMEM((8, 128, 128), F32),
            pltpu.VMEM((8, 128, 128), F32),
            pltpu.VMEM((8, 2, 128, 256), BF16),
            pltpu.VMEM((8, 128, 256), BF16),
            pltpu.SMEM((32,), jnp.int32),
        ],
        in_specs=[sm()] + [hbm()] * 5,
        out_specs=[vm()] * 4 + [sm()],
        scratch_shapes=[
            pltpu.VMEM((1024, 128), BF16), pltpu.VMEM((2048, 128), BF16), big(8, 256), big(8, 256),
            big(1024, 128), big(2048, 128), big(4, 256, 256), big(4, 128, 256), big(4, 8, 256),
            big(8, 128, 128), big(8, 128, 128),
            pltpu.VMEM((8, 128, 256), BF16), pltpu.VMEM((8, 128, 256), BF16),
            big(256, 128), big(256, 128),
            pltpu.SemaphoreType.DMA((5,)),
        ],
        compiler_params=pltpu.CompilerParams(vmem_limit_bytes=24 * 2**20),
        name="maps",
    )(tb, *[pltpu.with_memory_space_constraint(a, pltpu.HBM) for a in (slot_map, k, v, g, b)])


def final_kernel(pay_ref, keep_ref, got_ref, out_ref):
    def work(a_ref, m_ref):
        for h in range(8):
            out_ref[pl.ds(h * 64, 64), :] = mm_small(a_ref[h, :64], m_ref[h]) + a_ref[h, 64:]

    first = lax.axis_index("ctx") == 0

    @pl.when(first)
    def _():
        work(got_ref, pay_ref)

    @pl.when(jnp.logical_not(first))
    def _():
        work(keep_ref, got_ref)


def final(pay, keep, got):
    return pl.pallas_call(
        final_kernel,
        out_shape=pltpu.VMEM((512, 128), F32),
        in_specs=[vm(), vm(), vm()],
        out_specs=vm(),
        compiler_params=pltpu.CompilerParams(vmem_limit_bytes=16 * 2**20),
        name="final",
    )(pay, keep, got)


def reads_kernel(tb, q_ref, k_ref, v_ref, g_ref, b_ref, x_ref, l_ref, m_ref, o_ref, qf, kf, vf, rcol, bcol, ecol, of):
    qf[...] = q_ref[...].astype(F32)
    kf[...] = k_ref[...].astype(F32)
    vf[...] = v_ref[...].astype(F32)
    ctx = lax.axis_index("ctx")
    edge = tb[0] * 128 - ctx * 256
    live = lax.broadcasted_iota(jnp.int32, (8, 256), 1) < edge
    G = decay_rows(g_ref[...], live)
    lb = log_beta(b_ref[...])
    lane = lax.broadcasted_iota(jnp.int32, (256, 128), 1)
    norms = jnp.zeros((256, 128), F32)
    for kh in range(4):
        nk = log_norm(kf[pl.ds(kh, 256, stride=4), :])
        nq = log_norm(qf[pl.ds(kh, 256, stride=4), :])
        for h in (2 * kh, 2 * kh + 1):
            norms = jnp.where(lane == h, nk, norms)
            norms = jnp.where(lane == 8 + h, nq, norms)
    norm_rows = norms.T
    nk, nq = norm_rows[:8], norm_rows[8:16]
    p = G + nq
    a = G + nk + jnp.where(live, lb, -1e4)
    scale = to_columns(jnp.concatenate([jnp.exp(a), jnp.where(live, jnp.exp(lb), 0.0), jnp.exp(p)], axis=0))
    for h in range(8):
        rcol[h] = jnp.broadcast_to(scale[:, h : h + 1], (256, 128))
        bcol[h] = jnp.broadcast_to(scale[:, 8 + h : 9 + h], (256, 128))
        ecol[h] = jnp.broadcast_to(scale[:, 16 + h : 17 + h], (256, 128))
    cols, right = spans(p, G - nk)
    row = lax.broadcasted_iota(jnp.int32, (128, 128), 0)
    col = lax.broadcasted_iota(jnp.int32, (128, 128), 1)
    lower = row >= col
    has = (ctx != 0).astype(F32)
    live1, live2 = edge > 0, edge > 128
    def one(kh, c):
        k = kf[pl.ds(kh, 256, stride=4), :].astype(BF16)
        q = qf[pl.ds(kh, 256, stride=4), :].astype(BF16)
        qk1 = mm_nt(q[:128], k[:128])
        qk2 = mm_nt(q[128:], k)
        kq = jnp.concatenate([k, q], axis=0)
        for j in range(2):
            h = 2 * kh + j
            mrow = jnp.concatenate(split(m_ref[h] * has), axis=1)
            km = fold(mm(kq, mrow))
            d = bcol[h] * vf[pl.ds(h, 256, stride=8), :] - rcol[h] * km[:256]
            d1 = prod(x_ref[h, 0], pack_left(d[:128]))
            d2 = prod(x_ref[h, 1], pack_left(d[128:] - prod(l_ref[h], pack_left(d1))))
            qm = km[256:] * ecol[h]
            r = right(h)
            e1 = mm(cols[:128], r[:, :128])
            e2 = mm(cols[128:], r)
            p11 = jnp.where(lower, jnp.exp(e1) * qk1, 0.0)
            p21 = jnp.exp(e2[:, :128]) * qk2[:, :128]
            p22 = jnp.where(lower, jnp.exp(e2[:, 128:]) * qk2[:, 128:], 0.0)
            o1 = qm[:128] + mm_small(p11, d1)
            ph, pl_ = split(jnp.concatenate([p21, p22], axis=1))
            dh, dl = split(jnp.concatenate([d1, d2], axis=0))
            o2 = qm[128:] + fold(mm(ph, jnp.concatenate([dh, dl], axis=1))) + mm(pl_, dh)
            o1 = jnp.where(live1, o1, 0.0)
            o2 = jnp.where(live2, o2, 0.0)
            of[pl.ds(h, 256, stride=8), :] = jnp.concatenate([o1, o2], axis=0)
        return c

    lax.fori_loop(0, 4, one, 0)
    o_ref[...] = of[...].astype(BF16)


def reads(tb, q, k, v, g, b, x, l, m):
    big = lambda *s: pltpu.VMEM(s, F32)
    return pl.pallas_call(
        reads_kernel,
        out_shape=jax.ShapeDtypeStruct((2048, 128), BF16),
        in_specs=[sm()] + [vm()] * 8,
        out_specs=vm(),
        scratch_shapes=[
            big(1024, 128), big(1024, 128), big(2048, 128),
            big(8, 256, 128), big(8, 256, 128), big(8, 256, 128), big(2048, 128),
        ],
        compiler_params=pltpu.CompilerParams(vmem_limit_bytes=24 * 2**20),
        cost_estimate=pl.CostEstimate(flops=8 * 4 * 2 * 256**3, bytes_accessed=4 * 2**20, transcendentals=0),
        name="reads",
    )(tb, q, k, v, g, b, x, l, m)


def reorder_kernel(slot_ref, in_ref, out_ref):
    for s in range(32):
        out_ref[slot_ref[s]] = in_ref[s]


def reorder(slot_map, x):
    return pl.pallas_call(
        reorder_kernel,
        out_shape=pltpu.VMEM(x.shape, x.dtype),
        in_specs=[sm(), vm()],
        out_specs=vm(),
        name="reorder",
    )(
        pltpu.with_memory_space_constraint(slot_map, pltpu.SMEM),
        pltpu.with_memory_space_constraint(x, pltpu.VMEM),
    )


def place_kernel(in_ref, out_hbm, sem):
    copy = pltpu.make_async_copy(in_ref, out_hbm, sem)
    copy.start()
    copy.wait()


def place(x):
    return pl.pallas_call(
        place_kernel,
        out_shape=jax.ShapeDtypeStruct(x.shape, x.dtype),
        in_specs=[vm()],
        out_specs=hbm(),
        scratch_shapes=[pltpu.SemaphoreType.DMA],
        name="place",
    )(pltpu.with_memory_space_constraint(x, pltpu.VMEM))


def local(queries, keys, values, gate_logit, beta_logit, token_blocks, slot_map):
    q = queries.reshape(1024, 128)
    k = keys.reshape(1024, 128)
    v = values.reshape(2048, 128)
    g = gate_logit.reshape(8, 256)
    b = beta_logit.reshape(8, 256)
    pay, keep, x, l, slots = maps(token_blocks, slot_map, k, v, g, b)
    got = lax.ppermute(pay, "ctx", [(0, 1), (1, 0)])
    rows = final(pay, keep, got)
    spread = lax.all_to_all(rows.reshape(32, 16, 128), "sess", 0, 0, tiled=True)
    out = reads(token_blocks, q, k, v, g, b, x, l, got)
    back = lax.all_to_all(reorder(slots, spread), "sess", 0, 0, tiled=True)
    back = place(back.reshape(1, 8, 64, 128))
    return out.reshape(1, 256, 8, 128), back


def solution(mesh):
    from jax.sharding import PartitionSpec as P
    placed = (
        P("sess", "ctx", "head", None), P("sess", "ctx", "head", None), P("sess", "ctx", "head", None),
        P("sess", "head", "ctx"), P("sess", "head", "ctx"), P("sess"), P(),
    )
    return jax.shard_map(
        local, mesh=mesh, in_specs=placed,
        out_specs=(P("sess", "ctx", "head", None), P("sess", "head", "ctx", None)),
        check_vma=False,
    )
```
